256 devices in a mesh: seq: 32 (over z_lo, x, y), head: 8 (over z_hi, core).
Axes of the slice: x: 4, y: 4, z: 8 (z_hi: 4, z_lo: 2; z = z_hi * 2 + z_lo), core: 2. Of those that a mesh axis runs over, the one named last changes fastest.
Arguments:
- x_in: bfloat16 [16384, 4096], P('seq', 'head'), may hold values from -6 to 6
- b_proj: bfloat16 [16384, 1024], P('seq', 'head'), may hold values from -0.125 to 0.125
- c_proj: bfloat16 [16384, 1024], P('seq', 'head'), may hold values from -0.125 to 0.125
- decay: float32 [64, 16384], P('head', 'seq'), may hold values from 0.55 to 1, as said below
- d_skip: float32 [64], P('head'), may hold values from 0.5 to 1.5
- block_states: float32 [64, 64, 64, 128], P('seq', 'head'), may hold values from -6 to 6
- grad_out: bfloat16 [16384, 4096], P('seq', 'head'), may hold values from -6 to 6
- w_x: bfloat16 [4096, 4096], P(None, 'head'), may hold values from -0.09375 to 0.09375
- w_b: bfloat16 [4096, 1024], P(None, 'head'), may hold values from -0.09375 to 0.09375
- w_c: bfloat16 [4096, 1024], P(None, 'head'), may hold values from -0.09375 to 0.09375
Outputs:
- grad_input: bfloat16 [4096, 16384], P('head', 'seq')
- grad_decay: float32 [64, 16384], P('head', 'seq')
The draws below stay inside these ranges and needn't reach their ends.
Inputs may be any that keep to these rules, and one draw needn't show every extreme that they name: `decay`: on some heads the product of the decays over the whole sequence stays above a tenth; every other head loses half a percent or more at each step.
All inputs are finite; a program needn't handle non-finite values.
Results may differ from the reference program's by a relative error of at most 0.017.
Values may be sent and summed in bfloat16 or wider, within the bound.
A program may use at most 128 MiB of HBM per device.

```python
import math
import jax
import jax.numpy as jnp
from jax import lax

D = 4096
H = 64
P_SIZE = 64
N = 128
G = 8
Q = 256
TOK_DEV = 512
SEQUENCE_LENGTH = 16384
HEAD_SETS = 8


def draw_decay(key, part):
    key = jax.random.fold_in(key, 17)
    random_key_parts = jax.random.split(key, 6)
    fast_share = 0.5
    chooser = jax.random.uniform(random_key_parts[0], (H, 1))
    pace_slow = jnp.exp(jax.random.uniform(random_key_parts[1], (H, 1), minval=math.log(0.02 / SEQUENCE_LENGTH), maxval=math.log(0.2 / SEQUENCE_LENGTH)))
    rapid_speed = jnp.exp(jax.random.uniform(random_key_parts[2], (H, 1), minval=math.log(1.0 / 50.0), maxval=math.log(1.0 / 30.0)))
    pace = jnp.where(chooser < fast_share, rapid_speed, pace_slow)
    blocks = SEQUENCE_LENGTH // TOK_DEV
    factor = jnp.exp(jax.random.uniform(random_key_parts[3], (H, blocks), minval=math.log(0.5), maxval=math.log(2.0)))
    factor = jnp.repeat(factor, TOK_DEV, axis=1)
    jitter = jax.random.uniform(random_key_parts[4], (H, SEQUENCE_LENGTH), minval=0.5, maxval=1.5)
    spike_position = jax.random.randint(random_key_parts[5], (3,), 0, SEQUENCE_LENGTH)
    token_locations = jnp.arange(SEQUENCE_LENGTH)
    spike_events = jnp.any(token_locations[None, :] == spike_position[:, None], axis=0)
    kept_portion = jnp.where(spike_events, 0.65, 1.0)
    return (jnp.exp(-pace * factor * jitter) * kept_portion[None, :]).astype(jnp.float32)


def level_of(stream_key, extent, shards, low, top_value):
    loudness, own = 1.0, jax.random.fold_in(stream_key, 6)
    for position, shards_of in shards:
        heights = jnp.exp(jax.random.uniform(jax.random.fold_in(own, position), (shards_of,), jnp.float32, low / len(shards), top_value / len(shards)))
        loudness = loudness * jnp.repeat(heights, extent[position] // shards_of).reshape([-1 if axis == position else 1 for axis in range(len(extent))])
    return loudness


def centred(own_key, dims, scale, reach, cuts=(), held_as=jnp.bfloat16):
    entries = jax.random.normal(own_key, dims, jnp.float32) * scale
    if len(cuts) > 0:
        entries = level_of(own_key, dims, cuts, -0.22, 0.18) * entries
    return jnp.clip(entries, min=-reach, max=reach).astype(held_as)


def setup_inputs(seed: int = 0) -> dict:
    splits = jax.random.split(jax.random.key(seed), 11)
    x_in = centred(splits[0], (SEQUENCE_LENGTH, H * P_SIZE), 1.0, 6.0, ((0, 32), (1, 8)))
    b_proj = centred(splits[1], (SEQUENCE_LENGTH, G * N), (N * 16) ** -0.5, 0.125, ((0, 32), (1, 8)))
    c_proj = centred(splits[2], (SEQUENCE_LENGTH, G * N), (N * 16) ** -0.5, 0.125, ((0, 32), (1, 8)))
    decay = draw_decay(jax.random.fold_in(splits[10], 71), 0)
    d_skip = jnp.clip(0.5 + 1.0 * jax.random.uniform(splits[4], (H,), jnp.float32) ** level_of(splits[4], (H,), ((0, 8),), -0.2, 0.2), 0.5, 1.5)
    block_states = centred(splits[5], (SEQUENCE_LENGTH // Q, H, P_SIZE, N), 1.0, 6.0, ((0, 32), (1, 8)), jnp.float32)
    grad_out = centred(splits[6], (SEQUENCE_LENGTH, H * P_SIZE), 1.0, 6.0, ((0, 32), (1, 8)))
    w_x = centred(splits[7], (D, H * P_SIZE), D ** -0.5, 0.09375, ((1, 8),))
    w_b = centred(splits[8], (D, G * N), D ** -0.5, 0.09375, ((1, 8),))
    w_c = centred(splits[9], (D, G * N), D ** -0.5, 0.09375, ((1, 8),))
    return dict(x_in=x_in, b_proj=b_proj, c_proj=c_proj, decay=decay, d_skip=d_skip, block_states=block_states, grad_out=grad_out, w_x=w_x, w_b=w_b, w_c=w_c)


highest = lax.Precision.HIGHEST

def expand_groups(source, per_group):
    length, group_count, columns = source.shape
    return jnp.broadcast_to(source[:, :, None, :], (length, group_count, per_group, columns)).reshape(length, group_count * per_group, columns)

def suffix_sum(values):
    positions = jnp.arange(values.shape[-1])
    suffix_mask = (positions[:, None] >= positions[None, :]).astype(jnp.float32)
    return jnp.dot(values, suffix_mask, precision=highest)

def block_parts(inputs, upstream, b_rows, c_rows, log_decay, saved):
    head_count = inputs.shape[1]
    group_count = b_rows.shape[1]
    per_group = head_count // group_count
    block_len = inputs.shape[0]
    positions = jnp.arange(block_len)
    causal = positions[:, None] >= positions[None, :]
    cum_log = jnp.cumsum(log_decay, axis=1)
    log_gaps = cum_log[:, :, None] - cum_log[:, None, :]
    decay_mat = jnp.where(causal, jnp.exp(jnp.where(causal, log_gaps, 0.0)), 0.0)
    intersection = jnp.einsum('ign,jgn->gij', c_rows, b_rows, precision=highest)
    head_intersection = jnp.broadcast_to(intersection[:, None], (group_count, per_group, block_len, block_len)).reshape(head_count, block_len, block_len)
    b_heads = expand_groups(b_rows, per_group)
    c_heads = expand_groups(c_rows, per_group)
    forward_mat = decay_mat * head_intersection
    decayed_product = decay_mat * jnp.einsum('ihp,jhp->hij', upstream, inputs, precision=highest)
    from_start = jnp.exp(cum_log).T[:, :, None]
    to_end = jnp.exp(cum_log[:, -1:] - cum_log).T[:, :, None]
    grad_x0 = jnp.einsum('hij,ihp->jhp', forward_mat, upstream, precision=highest)
    grad_b0 = jnp.einsum('hij,ihn->jhn', decayed_product, c_heads, precision=highest)
    grad_c0 = jnp.einsum('hij,jhn->ihn', decayed_product, b_heads, precision=highest) + from_start * jnp.einsum('ihp,hpn->ihn', upstream, saved, precision=highest)
    output = jnp.einsum('hij,jhp->ihp', forward_mat, inputs, precision=highest) + from_start * jnp.einsum('ihn,hpn->ihp', c_heads, saved, precision=highest)
    terms_base = (lax.optimization_barrier(jnp.sum(upstream * output, axis=2)) - lax.optimization_barrier(jnp.sum(inputs * grad_x0, axis=2))).T
    adj_local = jnp.einsum('ihp,ihn->hpn', upstream * from_start, c_heads, precision=highest)
    coupling = jnp.einsum('ihp,ihn->hpn', inputs * to_end, b_heads, precision=highest)
    through = jnp.exp(cum_log[:, -1])
    return (grad_x0, grad_b0, grad_c0, terms_base, through, adj_local, coupling, to_end)

def right_terms(inputs, b_rows, to_end, adjoint):
    per_group = inputs.shape[1] // b_rows.shape[1]
    b_heads = expand_groups(b_rows, per_group)
    grad_xr = to_end * jnp.einsum('jhn,hpn->jhp', b_heads, adjoint, precision=highest)
    grad_br = to_end * jnp.einsum('jhp,hpn->jhn', inputs, adjoint, precision=highest)
    terms_right = -lax.optimization_barrier(jnp.sum(inputs * grad_xr, axis=2)).T
    return (grad_xr, grad_br, terms_right)

def reference(x_in, b_proj, c_proj, decay, d_skip, block_states, grad_out, w_x, w_b, w_c):
    blocks = SEQUENCE_LENGTH // Q
    inputs_all = x_in.reshape(blocks, Q, H, P_SIZE)
    upstream_all = grad_out.reshape(blocks, Q, H, P_SIZE)
    b_all = b_proj.reshape(blocks, Q, G, N)
    c_all = c_proj.reshape(blocks, Q, G, N)
    log_all = jnp.log(decay).reshape(H, blocks, Q).transpose(1, 0, 2)

    def sweep_block(carried, pieces):
        adjoint, later_total = carried
        x_blk, up_blk, b_blk, c_blk, log_blk, saved = pieces
        inputs = x_blk.astype(jnp.float32)
        upstream = up_blk.astype(jnp.float32)
        b_rows = b_blk.astype(jnp.float32)
        c_rows = c_blk.astype(jnp.float32)
        grad_x0, grad_b0, grad_c0, terms_base, through, adj_local, coupling, to_end = block_parts(inputs, upstream, b_rows, c_rows, log_blk, saved)
        grad_xr, grad_br, terms_right = right_terms(inputs, b_rows, to_end, adjoint)
        all_terms = terms_base + terms_right
        decay_grad = suffix_sum(all_terms) + later_total[:, None]
        grad_x = (grad_x0 + grad_xr + d_skip[None, :, None] * upstream).reshape(Q, H * P_SIZE).astype(jnp.bfloat16)
        grad_b = (grad_b0 + grad_br).reshape(Q, G, H // G, N).sum(axis=2).reshape(Q, G * N).astype(jnp.bfloat16)
        grad_c = grad_c0.reshape(Q, G, H // G, N).sum(axis=2).reshape(Q, G * N).astype(jnp.bfloat16)
        new_adjoint = adj_local + through[:, None, None] * adjoint
        new_total = later_total + lax.optimization_barrier(jnp.sum(all_terms, axis=1))
        return ((new_adjoint, new_total), (grad_x, grad_b, grad_c, decay_grad))
    initial = (jnp.zeros((H, P_SIZE, N), jnp.float32), jnp.zeros((H,), jnp.float32))
    finished, results = lax.scan(sweep_block, initial, (inputs_all, upstream_all, b_all, c_all, log_all, block_states), reverse=True)
    grad_x, grad_b, grad_c, decay_grad = results
    grad_x = grad_x.reshape(SEQUENCE_LENGTH, H * P_SIZE)
    grad_b = grad_b.reshape(SEQUENCE_LENGTH, G * N)
    grad_c = grad_c.reshape(SEQUENCE_LENGTH, G * N)
    x_width = H * P_SIZE // HEAD_SETS
    g_width = G * N // HEAD_SETS
    summed = jnp.zeros((D, SEQUENCE_LENGTH), jnp.float32)
    for index_s in range(HEAD_SETS):
        x_lo = index_s * x_width
        g_lo = index_s * g_width
        partial_value = jnp.dot(w_x[:, x_lo:x_lo + x_width], grad_x[:, x_lo:x_lo + x_width].T, preferred_element_type=jnp.float32)
        partial_value = partial_value + jnp.dot(w_b[:, g_lo:g_lo + g_width], grad_b[:, g_lo:g_lo + g_width].T, preferred_element_type=jnp.float32)
        partial_value = partial_value + jnp.dot(w_c[:, g_lo:g_lo + g_width], grad_c[:, g_lo:g_lo + g_width].T, preferred_element_type=jnp.float32)
        rounded = lax.optimization_barrier(partial_value.astype(jnp.bfloat16))
        summed = summed + rounded.astype(jnp.float32)
    norm_factor = 1.0 / math.sqrt(SEQUENCE_LENGTH)
    grad_decay = decay_grad.transpose(1, 0, 2).reshape(H, SEQUENCE_LENGTH) * norm_factor
    return (summed.astype(jnp.bfloat16), grad_decay)
```

```python
import math

import jax
import jax.numpy as jnp
from jax import lax
from jax.experimental import pallas as pl
from jax.experimental.pallas import tpu as pltpu
from jax.sharding import PartitionSpec as P

SEQ = 32
HEAD = 8
TOK = 512
Q = 256
NH = 8
PS = 64
N = 128
HP = NH * PS
KOWN = HP + 2 * N
ROWS = 512
TM = 128
SL = HP // SEQ

MESH = pl.DeviceIdType.MESH
f32 = jnp.float32
bf16 = jnp.bfloat16

TN = (((0,), (0,)), ((), ()))
NT = (((1,), (1,)), ((), ()))


def dot(a, b, dims=(((1,), (0,)), ((), ()))):
    return lax.dot_general(a, b, dims, preferred_element_type=f32)


def split3(v):
    hi = v.astype(bf16).astype(f32)
    rest = v - hi
    mid = rest.astype(bf16).astype(f32)
    low = rest - mid
    return jnp.concatenate([hi, mid, low], axis=0).astype(bf16)


def exact_dot(v, mask):
    rows = v.shape[0]
    out = dot(split3(v), mask)
    return out[0:rows] + out[rows : 2 * rows] + out[2 * rows : 3 * rows]


def kernel(
    x_hbm, b_hbm, c_hbm, dec_hbm, skip_ref, st_hbm, dy_hbm, wx_hbm, wb_hbm, wc_hbm,
    out_hbm, gd_ref,
    x_v, b_v, c_v, dec_v, st_v, dy_v, w_v, g_v,
    xt, dyt, bt, ct, xte, dyfs, cum_s, cumt_s, fs_s, te_s, th_s,
    adj1, summ, ra, rt, ob, a_v, tt_s,
    gx, gb, wd, cb, yi, terms, rt2, tsum,
    sl, rl, sr, rr, own, acc, o_v,
    load_sem, w_sem, g_sem, a_send, a_recv, rs_l, rs_r, out_sem,
):
    s = lax.axis_index("seq")
    h = lax.axis_index("head")
    z = h // 2
    core = lax.rem(h, 2)
    sib = (s, h + 1 - 2 * core)
    left = (s, lax.rem(h + HEAD - 2, HEAD))
    right = (s, lax.rem(h + 2, HEAD))

    def peer(o):
        return (lax.rem(s + o, SEQ), h)

    barrier = pltpu.get_barrier_semaphore()

    def greet(o, carry):
        pl.semaphore_signal(barrier, inc=1, device_id=peer(o), device_id_type=MESH)
        return carry

    lax.fori_loop(1, SEQ, greet, 0)
    for other in (sib, left, right):
        pl.semaphore_signal(barrier, inc=1, device_id=other, device_id_type=MESH)

    loads = [
        pltpu.make_async_copy(src, dst, load_sem.at[i])
        for i, (src, dst) in enumerate(
            (
                (dec_hbm, dec_v),
                (dy_hbm, dy_v),
                (c_hbm, c_v),
                (b_hbm, b_v),
                (x_hbm, x_v),
                (st_hbm, st_v),
                (wx_hbm.at[:, core], w_v.at[:, :, 0:HP]),
                (wb_hbm.at[:, core], w_v.at[:, :, HP : HP + N]),
                (wc_hbm.at[:, core], w_v.at[:, :, HP + N : KOWN]),
            )
        )
    ]
    for load in loads:
        load.start()

    row_i = lax.broadcasted_iota(jnp.int32, (Q, Q), 0)
    col_i = lax.broadcasted_iota(jnp.int32, (Q, Q), 1)

    loads[0].wait()
    upto = (row_i <= col_i).astype(f32).astype(bf16)
    log_decay = jnp.log(dec_v[...])
    for k in range(2):
        lanes = slice(k * Q, (k + 1) * Q)
        cum = exact_dot(log_decay[:, lanes], upto)
        cum_s[:, lanes] = cum
        fs_s[:, lanes] = jnp.exp(cum)
        last = jnp.broadcast_to(cum[:, Q - 1 : Q], (NH, Q))
        te_s[:, lanes] = jnp.exp(last - cum)
        th_s[k] = jnp.exp(last[:, 0:N])
    tt_s[...] = th_s[0] * th_s[1]
    rt[0] = tt_s[...]

    loads[1].wait()
    dyt[...] = dy_v[...].T
    for i in range(NH):
        rows = slice(i * PS, (i + 1) * PS)
        dyfs[rows, :] = (dyt[rows, :].astype(f32) * fs_s[i : i + 1, :]).astype(bf16)
    loads[2].wait()
    adj1[...] = dot(dyfs[:, Q : 2 * Q], c_v[Q : 2 * Q, :])
    adj0 = dot(dyfs[:, 0:Q], c_v[0:Q, :])
    for i in range(NH):
        rows = slice(i * PS, (i + 1) * PS)
        summ[rows, :] = (adj0[rows, :] + th_s[0, i : i + 1, :] * adj1[rows, :]).astype(bf16)
    ra[0] = summ[pl.ds(pl.multiple_of(s * SL, SL), SL), :]

    pl.semaphore_wait(barrier, SEQ - 1 + 3)

    def send_slice(o, carry):
        to = lax.rem(s + o, SEQ)
        pltpu.make_async_remote_copy(
            src_ref=summ.at[pl.ds(pl.multiple_of(to * SL, SL), SL)],
            dst_ref=ra.at[SEQ - o],
            send_sem=a_send.at[0],
            recv_sem=a_recv.at[0],
            device_id=(to, h),
            device_id_type=MESH,
        ).start()
        pltpu.make_async_remote_copy(
            src_ref=tt_s,
            dst_ref=rt.at[SEQ - o],
            send_sem=a_send.at[1],
            recv_sem=a_recv.at[1],
            device_id=(to, h),
            device_id_type=MESH,
        ).start()
        return carry

    lax.fori_loop(1, SEQ, send_slice, 0)

    w_copies = [
        pltpu.make_async_remote_copy(
            src_ref=src.at[:, 1 - core],
            dst_ref=w_v.at[:, :, lo:hi],
            send_sem=w_sem.at[0, i],
            recv_sem=w_sem.at[1, i],
            device_id=sib,
            device_id_type=MESH,
        )
        for i, (src, lo, hi) in enumerate(
            (
                (wx_hbm, KOWN, KOWN + HP),
                (wb_hbm, KOWN + HP, KOWN + HP + N),
                (wc_hbm, KOWN + HP + N, 2 * KOWN),
            )
        )
    ]
    for copy in w_copies:
        copy.start()

    loads[4].wait()
    xt[...] = x_v[...].T
    for i in range(NH):
        rows = slice(i * PS, (i + 1) * PS)
        xte[rows, :] = (xt[rows, :].astype(f32) * te_s[i : i + 1, :]).astype(bf16)
    loads[3].wait()
    bt[...] = b_v[...].T
    ct[...] = c_v[...].T
    cumt_s[...] = cum_s[...].T
    loads[5].wait()

    def all_of(ref, i):
        return pltpu.make_async_remote_copy(
            src_ref=ref,
            dst_ref=ref,
            send_sem=a_send.at[i],
            recv_sem=a_recv.at[i],
            device_id=sib,
            device_id_type=MESH,
        )

    for i, ref in ((0, ra), (1, rt)):
        arrived = all_of(ref.at[pl.ds(1, SEQ - 1)], i)
        arrived.wait_recv()
    mine = s // (SEQ // NH)

    def scan(step, cur):
        d = SEQ - 1 - step
        slot = lax.rem(d - s + SEQ, SEQ)
        ob[d] = cur.astype(bf16)
        through = rt[slot, pl.ds(mine, 1), :]
        return ra[slot].astype(f32) + through * cur

    lax.fori_loop(0, SEQ, scan, jnp.zeros((SL, N), f32))
    own_rows = pl.ds(pl.multiple_of(s * SL, SL), SL)
    a_v[own_rows, :] = ob[s]

    def send_back(o, carry):
        to = lax.rem(s + o, SEQ)
        pltpu.make_async_remote_copy(
            src_ref=ob.at[to],
            dst_ref=a_v.at[own_rows],
            send_sem=a_send.at[2],
            recv_sem=a_recv.at[2],
            device_id=(to, h),
            device_id_type=MESH,
        ).start()
        return carry

    lax.fori_loop(1, SEQ, send_back, 0)

    def block(k, carry):
        lanes = pl.ds(pl.multiple_of(k * Q, Q), Q)
        srows = pl.ds(pl.multiple_of(k * HP, HP), HP)
        c_k = c_v[lanes, :]
        bt_k = bt[:, lanes]
        ct_k = ct[:, lanes]
        s0 = st_v[srows, :].astype(bf16)
        cb[...] = dot(c_k, bt_k)
        yi[...] = dot(s0, ct_k)
        causal = row_i >= col_i
        for i in range(NH):
            rows = slice(i * PS, (i + 1) * PS)
            xh = xt[rows, lanes]
            dyh = dyt[rows, lanes]
            gaps = cumt_s[lanes, i : i + 1] - cum_s[i : i + 1, lanes]
            decay = jnp.exp(jnp.where(causal, gaps, -1e30))
            forward = (decay * cb[...]).astype(bf16)
            product = dot(dy_v[lanes, rows], xh)
            if i == 0:
                wd[...] = decay * product
            else:
                wd[...] += decay * product
            gx0 = dot(dyh, forward)
            y = dot(xh, forward, NT) + fs_s[i : i + 1, lanes] * yi[rows, :]
            dyf = dyh.astype(f32)
            terms[i : i + 1, lanes] = jnp.sum(dyf * y - xh.astype(f32) * gx0, axis=0, keepdims=True)
            gx[rows, lanes] = gx0 + skip_ref[i] * dyf
        decayed = wd[...].astype(bf16)
        gb[:, lanes] = dot(ct_k, decayed)
        gc = dot(bt_k, decayed, NT) + dot(s0, dyfs[:, lanes], TN)
        g_v[HP + N : KOWN, lanes] = gc.astype(bf16)
        return carry

    lax.fori_loop(0, 2, block, 0)

    all_of(a_v.at[pl.ds(0, HP - SL)], 2).wait_recv()
    later = a_v[...]
    for k in (1, 0):
        lanes = slice(k * Q, (k + 1) * Q)
        if k == 0:
            later = jnp.concatenate(
                [
                    (
                        adj1[i * PS : (i + 1) * PS, :]
                        + th_s[1, i : i + 1, :] * a_v[i * PS : (i + 1) * PS, :].astype(f32)
                    ).astype(bf16)
                    for i in range(NH)
                ],
                axis=0,
            )
        yi[...] = dot(later, bt[:, lanes])
        g_v[HP : HP + N, lanes] = (gb[:, lanes] + dot(later, xte[:, lanes], TN)).astype(bf16)
        for i in range(NH):
            rows = slice(i * PS, (i + 1) * PS)
            gxr = te_s[i : i + 1, lanes] * yi[rows, :]
            g_v[rows, lanes] = (gx[rows, lanes] + gxr).astype(bf16)
            terms[i : i + 1, lanes] -= jnp.sum(
                xt[rows, lanes].astype(f32) * gxr, axis=0, keepdims=True
            )

    g_copy = pltpu.make_async_remote_copy(
        src_ref=g_v.at[pl.ds(0, KOWN)],
        dst_ref=g_v.at[pl.ds(KOWN, KOWN)],
        send_sem=g_sem.at[0],
        recv_sem=g_sem.at[1],
        device_id=sib,
        device_id_type=MESH,
    )
    g_copy.start()

    for load in loads[6:]:
        load.wait()
    for copy in w_copies:
        copy.wait()
    g_copy.wait()

    def product_of(chunk, row):
        return dot(w_v[chunk, pl.ds(pl.multiple_of(row, TM), TM), :], g_v[...])

    ahead = lax.rem(z + 1, 4)
    behind = lax.rem(z + 3, 4)
    far = lax.rem(z + 2, 4)

    def to_left(stage, j):
        return pltpu.make_async_remote_copy(
            src_ref=sl.at[stage, j],
            dst_ref=rl.at[stage, j],
            send_sem=rs_l.at[0, stage, j],
            recv_sem=rs_l.at[1, stage, j],
            device_id=left,
            device_id_type=MESH,
        )

    def to_right(stage, j):
        return pltpu.make_async_remote_copy(
            src_ref=sr.at[stage, j],
            dst_ref=rr.at[stage, j],
            send_sem=rs_r.at[0, stage, j],
            recv_sem=rs_r.at[1, stage, j],
            device_id=right,
            device_id_type=MESH,
        )

    def far_tiles(j, carry):
        sl[0, j] = product_of(far, j * TM).astype(bf16)
        to_left(0, j).start()
        sr[0, j] = product_of(far, 2 * TM + j * TM).astype(bf16)
        to_right(0, j).start()
        return carry

    lax.fori_loop(0, 2, far_tiles, 0)

    def direct_tiles(j, carry):
        sl[1, j] = product_of(behind, 2 * TM + j * TM).astype(bf16)
        to_left(1, j).start()
        sr[1, j] = product_of(ahead, j * TM).astype(bf16)
        to_right(1, j).start()
        return carry

    lax.fori_loop(0, 2, direct_tiles, 0)

    from_on = (row_i >= col_i).astype(f32).astype(bf16)
    suffix = [exact_dot(terms[:, k * Q : (k + 1) * Q], from_on) for k in range(2)]
    first, second = (jnp.broadcast_to(part[:, 0:1], (NH, N)) for part in suffix)
    tsum[...] = first + second

    def send_sum(o, carry):
        pltpu.make_async_remote_copy(
            src_ref=tsum,
            dst_ref=rt2.at[SEQ - o],
            send_sem=a_send.at[3],
            recv_sem=a_recv.at[3],
            device_id=peer(o),
            device_id_type=MESH,
        ).start()
        return carry

    lax.fori_loop(1, SEQ, send_sum, 0)

    def next_tiles(j, carry):
        acc[0, j] = product_of(behind, j * TM)
        acc[1, j] = product_of(ahead, 2 * TM + j * TM)
        return carry

    lax.fori_loop(0, 2, next_tiles, 0)

    def own_tiles(j, carry):
        own[j] = product_of(z, j * TM)
        return carry

    lax.fori_loop(0, 4, own_tiles, 0)

    for j in range(2):
        to_left(0, j).wait_recv()
        sl[2, j] = (acc[0, j] + rl[0, j].astype(f32)).astype(bf16)
        to_left(2, j).start()
        to_right(0, j).wait_recv()
        sr[2, j] = (acc[1, j] + rr[0, j].astype(f32)).astype(bf16)
        to_right(2, j).start()

    all_of(rt2.at[pl.ds(1, SEQ - 1)], 3).wait_recv()

    def add_later(o, total):
        return total + jnp.where(s + o < SEQ, rt2[o], 0.0)

    running = lax.fori_loop(1, SEQ, add_later, jnp.zeros((NH, N), f32))
    norm = 1.0 / math.sqrt(SEQ * TOK)
    gd_ref[:, Q : 2 * Q] = (suffix[1] + running[:, 0:1]) * norm
    gd_ref[:, 0:Q] = (suffix[0] + (running + second)[:, 0:1]) * norm

    outs = []
    for j in range(2):
        to_right(1, j).wait_recv()
        to_left(2, j).wait_recv()
        a_tile = own[j] + rr[1, j].astype(f32) + rl[2, j].astype(f32)
        o_v[j * TM : (j + 1) * TM, :] = a_tile.astype(bf16)
        to_left(1, j).wait_recv()
        to_right(2, j).wait_recv()
        b_tile = own[2 + j] + rl[1, j].astype(f32) + rr[2, j].astype(f32)
        o_v[(2 + j) * TM : (3 + j) * TM, :] = b_tile.astype(bf16)
        for half in (j, 2 + j):
            rows = pl.ds(half * TM, TM)
            copy = pltpu.make_async_copy(o_v.at[rows], out_hbm.at[rows], out_sem.at[half])
            copy.start()
            outs.append(copy)

    for i, ref in (
        (0, ra.at[pl.ds(1, SEQ - 1)]),
        (1, rt.at[pl.ds(1, SEQ - 1)]),
        (2, ob.at[pl.ds(1, SEQ - 1)]),
        (3, rt2.at[pl.ds(1, SEQ - 1)]),
    ):
        all_of(ref, i).wait_send()
    for stage in range(3):
        for j in range(2):
            to_left(stage, j).wait_send()
            to_right(stage, j).wait_send()
    for copy in outs:
        copy.wait()


def body(x_in, b_proj, c_proj, decay, d_skip, block_states, grad_out, w_x, w_b, w_c):
    any_spec = pl.BlockSpec(memory_space=pl.ANY)
    dma = pltpu.SemaphoreType.DMA
    return pl.pallas_call(
        kernel,
        out_shape=(
            jax.ShapeDtypeStruct((ROWS, TOK), bf16),
            jax.ShapeDtypeStruct((NH, TOK), f32),
        ),
        in_specs=[any_spec] * 4 + [pl.BlockSpec(memory_space=pltpu.SMEM)] + [any_spec] * 5,
        out_specs=(any_spec, pl.BlockSpec(memory_space=pltpu.VMEM)),
        scratch_shapes=[
            pltpu.VMEM((TOK, HP), bf16),
            pltpu.VMEM((TOK, N), bf16),
            pltpu.VMEM((TOK, N), bf16),
            pltpu.VMEM((NH, TOK), f32),
            pltpu.VMEM((2 * HP, N), f32),
            pltpu.VMEM((TOK, HP), bf16),
            pltpu.VMEM((4, ROWS, 2 * KOWN), bf16),
            pltpu.VMEM((2 * KOWN, TOK), bf16),
            pltpu.VMEM((HP, TOK), bf16),
            pltpu.VMEM((HP, TOK), bf16),
            pltpu.VMEM((N, TOK), bf16),
            pltpu.VMEM((N, TOK), bf16),
            pltpu.VMEM((HP, TOK), bf16),
            pltpu.VMEM((HP, TOK), bf16),
            pltpu.VMEM((NH, TOK), f32),
            pltpu.VMEM((TOK, NH), f32),
            pltpu.VMEM((NH, TOK), f32),
            pltpu.VMEM((NH, TOK), f32),
            pltpu.VMEM((2, NH, N), f32),
            pltpu.VMEM((HP, N), f32),
            pltpu.VMEM((HP, N), bf16),
            pltpu.VMEM((SEQ, SL, N), bf16),
            pltpu.VMEM((SEQ, NH, N), f32),
            pltpu.VMEM((SEQ, SL, N), bf16),
            pltpu.VMEM((HP, N), bf16),
            pltpu.VMEM((NH, N), f32),
            pltpu.VMEM((HP, TOK), f32),
            pltpu.VMEM((N, TOK), f32),
            pltpu.VMEM((Q, Q), f32),
            pltpu.VMEM((Q, Q), f32),
            pltpu.VMEM((HP, Q), f32),
            pltpu.VMEM((NH, TOK), f32),
            pltpu.VMEM((SEQ, NH, N), f32),
            pltpu.VMEM((NH, N), f32),
            pltpu.VMEM((3, 2, TM, TOK), bf16),
            pltpu.VMEM((3, 2, TM, TOK), bf16),
            pltpu.VMEM((3, 2, TM, TOK), bf16),
            pltpu.VMEM((3, 2, TM, TOK), bf16),
            pltpu.VMEM((4, TM, TOK), f32),
            pltpu.VMEM((2, 2, TM, TOK), f32),
            pltpu.VMEM((ROWS, TOK), bf16),
            dma((9,)),
            dma((2, 3)),
            dma((2,)),
            dma((4,)),
            dma((4,)),
            dma((2, 3, 2)),
            dma((2, 3, 2)),
            dma((4,)),
        ],
        compiler_params=pltpu.CompilerParams(
            collective_id=0, has_side_effects=True, vmem_limit_bytes=48 * 2**20
        ),
    )(
        x_in,
        b_proj,
        c_proj,
        decay,
        d_skip,
        block_states.reshape(2 * HP, N),
        grad_out,
        w_x.reshape(4, 2, ROWS, HP),
        w_b.reshape(4, 2, ROWS, N),
        w_c.reshape(4, 2, ROWS, N),
    )


def solution(mesh):
    return jax.shard_map(
        body,
        mesh=mesh,
        in_specs=(
            P("seq", "head"),
            P("seq", "head"),
            P("seq", "head"),
            P("head", "seq"),
            P("head"),
            P("seq", "head", None, None),
            P("seq", "head"),
            P(None, "head"),
            P(None, "head"),
            P(None, "head"),
        ),
        out_specs=(P("head", "seq"), P("head", "seq")),
        check_vma=False,
    )
```

```python
import math

import jax
import jax.numpy as jnp
from jax import lax
from jax.experimental import pallas as pl
from jax.experimental.pallas import tpu as pltpu
from jax.sharding import PartitionSpec as P

SEQ = 32
HEAD = 8
TOK = 512
Q = 256
NH = 8
PS = 64
N = 128
HP = NH * PS
KOWN = HP + 2 * N
ROWS = 512
TM = 128
SL = HP // SEQ

MESH = pl.DeviceIdType.MESH
f32 = jnp.float32
bf16 = jnp.bfloat16

TN = (((0,), (0,)), ((), ()))
NT = (((1,), (1,)), ((), ()))


def dot(a, b, dims=(((1,), (0,)), ((), ()))):
    return lax.dot_general(a, b, dims, preferred_element_type=f32)


def split3(v):
    hi = v.astype(bf16).astype(f32)
    rest = v - hi
    mid = rest.astype(bf16).astype(f32)
    low = rest - mid
    return jnp.concatenate([hi, mid, low], axis=0).astype(bf16)


def exact_dot(v, mask):
    rows = v.shape[0]
    out = dot(split3(v), mask)
    return out[0:rows] + out[rows : 2 * rows] + out[2 * rows : 3 * rows]


def kernel(
    x_hbm, b_hbm, c_hbm, dec_hbm, skip_hbm, st_hbm, dy_hbm, wx_hbm, wb_hbm, wc_hbm,
    out_hbm, gd_hbm,
    x_v, b_v, c_v, dec_v, st_v, dy_v, w_v, g_v,
    xt, dyt, bt, ct, xte, dyfs, cum_s, cumt_s, fs_s, te_s, th0, th1,
    adj1, msg, ra, ob, a_v,
    gx, gb, wd, cb, yi, r_s, terms, rt2, tsum, run_v,
    sl, rl, sr, rr, own, acc, o_v, gd_v, skip_ref,
    load_sem, w_sem, p_sem, a_send, a_recv, rs_l, rs_r, out_sem,
):
    s = lax.axis_index("seq")
    h = lax.axis_index("head")
    z = h // 2
    core = lax.rem(h, 2)
    sib = (s, h + 1 - 2 * core)
    left = (s, lax.rem(h + HEAD - 2, HEAD))
    right = (s, lax.rem(h + 2, HEAD))

    def peer(o):
        return (lax.rem(s + o, SEQ), sib[1])

    barrier = pltpu.get_barrier_semaphore()

    def greet(o, carry):
        pl.semaphore_signal(barrier, inc=1, device_id=peer(o), device_id_type=MESH)
        return carry

    lax.fori_loop(0, SEQ, greet, 0)
    for other in (left, right):
        pl.semaphore_signal(barrier, inc=1, device_id=other, device_id_type=MESH)

    loads = [
        pltpu.make_async_copy(src, dst, load_sem.at[i])
        for i, (src, dst) in enumerate(
            (
                (dec_hbm, dec_v),
                (dy_hbm, dy_v),
                (c_hbm, c_v),
                (b_hbm, b_v),
                (x_hbm, x_v),
                (st_hbm, st_v),
                (wx_hbm.at[:, core], w_v.at[:, :, 0:HP]),
                (wb_hbm.at[:, core], w_v.at[:, :, HP : HP + N]),
                (wc_hbm.at[:, core], w_v.at[:, :, HP + N : KOWN]),
                (skip_hbm, skip_ref),
            )
        )
    ]
    for load in loads:
        load.start()

    row_i = lax.broadcasted_iota(jnp.int32, (Q, Q), 0)
    col_i = lax.broadcasted_iota(jnp.int32, (Q, Q), 1)

    loads[0].wait()
    upto = (row_i <= col_i).astype(f32).astype(bf16)
    log_decay = jnp.log(dec_v[...])
    for k in range(2):
        lanes = slice(k * Q, (k + 1) * Q)
        cum = exact_dot(log_decay[:, lanes], upto)
        cum_s[:, lanes] = cum
        fs_s[:, lanes] = jnp.exp(cum)
        last = jnp.broadcast_to(cum[:, Q - 1 : Q], (NH, Q))
        te_s[0, :, lanes] = jnp.exp(last - cum)
        (th0, th1.at[0])[k][...] = jnp.exp(last[:, 0:N])
    through = th0[...] * th1[0]
    coarse = through.astype(bf16).astype(f32)
    fine = through - coarse
    factors = [
        jnp.concatenate(
            [jnp.broadcast_to(part[i : i + 1, :], (SL // 2, N)) for part in (coarse, fine)], axis=0
        ).astype(bf16)
        for i in range(NH)
    ]

    loads[1].wait()
    dyt[...] = dy_v[...].T
    for i in range(NH):
        rows = slice(i * PS, (i + 1) * PS)
        dyfs[rows, :] = (dyt[rows, :].astype(f32) * fs_s[i : i + 1, :]).astype(bf16)
    loads[2].wait()
    adj1[0] = dot(dyfs[:, Q : 2 * Q], c_v[Q : 2 * Q, :])
    adj0 = dot(dyfs[:, 0:Q], c_v[0:Q, :])
    for i in range(SEQ):
        rows = slice(i * SL, (i + 1) * SL)
        head = i * SL // PS
        msg[i, 0:SL] = (adj0[rows, :] + th0[head : head + 1, :] * adj1[0, rows, :]).astype(bf16)
        msg[i, SL : 2 * SL] = factors[head]

    pl.semaphore_wait(barrier, SEQ + 2)

    def send_slice(o, carry):
        to = lax.rem(s + o, SEQ)
        pltpu.make_async_remote_copy(
            src_ref=msg.at[to],
            dst_ref=ra.at[lax.rem(SEQ - o, SEQ)],
            send_sem=a_send.at[0],
            recv_sem=a_recv.at[0],
            device_id=(to, sib[1]),
            device_id_type=MESH,
        ).start()
        return carry

    lax.fori_loop(0, SEQ, send_slice, 0)

    def to_sib(src, dst, sems, i):
        return pltpu.make_async_remote_copy(
            src_ref=src,
            dst_ref=dst,
            send_sem=sems.at[0, i],
            recv_sem=sems.at[1, i],
            device_id=sib,
            device_id_type=MESH,
        )

    w_copies = [
        to_sib(src.at[:, 1 - core], w_v.at[:, :, lo:hi], w_sem, i)
        for i, (src, lo, hi) in enumerate(
            (
                (wx_hbm, KOWN, KOWN + HP),
                (wb_hbm, KOWN + HP, KOWN + HP + N),
                (wc_hbm, KOWN + HP + N, 2 * KOWN),
            )
        )
    ]
    early = [
        to_sib(ref.at[0], ref.at[1], p_sem, i) for i, ref in enumerate((te_s, th1, adj1, bt, xte))
    ]
    for copy in w_copies:
        copy.start()

    loads[4].wait()
    xt[...] = x_v[...].T
    for i in range(NH):
        rows = slice(i * PS, (i + 1) * PS)
        xte[0, rows, :] = (xt[rows, :].astype(f32) * te_s[0, i : i + 1, :]).astype(bf16)
    loads[3].wait()
    bt[0] = b_v[...].T
    ct[...] = c_v[...].T
    cumt_s[...] = cum_s[...].T

    loads[5].wait()
    loads[9].wait()
    def block(k, carry):
        lanes = pl.ds(pl.multiple_of(k * Q, Q), Q)
        srows = pl.ds(pl.multiple_of(k * HP, HP), HP)
        c_k = c_v[lanes, :]
        bt_k = bt[0, :, lanes]
        ct_k = ct[:, lanes]
        s0 = st_v[srows, :].astype(bf16)
        cb[...] = dot(c_k, bt_k)
        yi[...] = dot(s0, ct_k)
        causal = row_i >= col_i
        for i in range(NH):
            rows = slice(i * PS, (i + 1) * PS)
            xh = xt[rows, lanes]
            dyh = dyt[rows, lanes]
            gaps = cumt_s[lanes, i : i + 1] - cum_s[i : i + 1, lanes]
            decay = jnp.exp(jnp.where(causal, gaps, -1e30))
            forward = (decay * cb[...]).astype(bf16)
            product = dot(dy_v[lanes, rows], xh)
            if i == 0:
                wd[...] = decay * product
            else:
                wd[...] += decay * product
            gx0 = dot(dyh, forward)
            y = dot(xh, forward, NT) + fs_s[i : i + 1, lanes] * yi[rows, :]
            dyf = dyh.astype(f32)
            terms[i : i + 1, lanes] = jnp.sum(dyf * y - xh.astype(f32) * gx0, axis=0, keepdims=True)
            gx[0, rows, lanes] = gx0 + skip_ref[i] * dyf
        decayed = wd[...].astype(bf16)
        gb[0, :, lanes] = dot(ct_k, decayed)
        gc = dot(bt_k, decayed, NT) + dot(s0, dyfs[:, lanes], TN)
        g_v[HP + N : KOWN, lanes] = gc.astype(bf16)
        return carry

    for copy in early:
        copy.start()
    lax.fori_loop(0, 2, block, 0)

    late = [
        to_sib(src, dst, p_sem, 5 + i)
        for i, (src, dst) in enumerate(
            (
                (gx.at[0], gx.at[1]),
                (gb.at[0], gb.at[1]),
                (g_v.at[pl.ds(HP + N, N)], g_v.at[pl.ds(KOWN + HP + N, N)]),
            )
        )
    ]
    for copy in late:
        copy.start()

    def all_of(ref, i):
        return pltpu.make_async_remote_copy(
            src_ref=ref,
            dst_ref=ref,
            send_sem=a_send.at[i],
            recv_sem=a_recv.at[i],
            device_id=sib,
            device_id_type=MESH,
        )

    all_of(ra, 0).wait_recv()

    def scan(step, cur):
        d = SEQ - 1 - step
        slot = lax.rem(d - s + SEQ, SEQ)
        ob[d] = cur.astype(bf16)
        parts = ra[slot, SL : 2 * SL, :].astype(f32)
        factor = parts[0 : SL // 2, :] + parts[SL // 2 : SL, :]
        return ra[slot, 0:SL, :].astype(f32) + jnp.concatenate([factor, factor], axis=0) * cur

    lax.fori_loop(0, SEQ, scan, jnp.zeros((SL, N), f32))
    own_rows = pl.ds(pl.multiple_of(s * SL, SL), SL)

    def send_back(o, carry):
        to = lax.rem(s + o, SEQ)
        pltpu.make_async_remote_copy(
            src_ref=ob.at[to],
            dst_ref=a_v.at[0, own_rows],
            send_sem=a_send.at[1],
            recv_sem=a_recv.at[1],
            device_id=(to, sib[1]),
            device_id_type=MESH,
        ).start()
        return carry

    lax.fori_loop(0, SEQ, send_back, 0)

    all_of(a_v.at[0], 1).wait_recv()
    a_copy = to_sib(a_v.at[0], a_v.at[1], p_sem, 8)
    a_copy.start()

    def with_adjoint(side):
        for k in (1, 0):
            lanes = slice(k * Q, (k + 1) * Q)
            later = a_v[side]
            if k == 0:
                later = jnp.concatenate(
                    [
                        (
                            adj1[side, i * PS : (i + 1) * PS, :]
                            + th1[side, i : i + 1, :]
                            * a_v[side, i * PS : (i + 1) * PS, :].astype(f32)
                        ).astype(bf16)
                        for i in range(NH)
                    ],
                    axis=0,
                )
            r_s[side, :, lanes] = dot(later, bt[side, :, lanes])
            base = side * KOWN
            g_v[base + HP : base + HP + N, lanes] = (
                gb[side, :, lanes] + dot(later, xte[side, :, lanes], TN)
            ).astype(bf16)
            for i in range(NH):
                rows = slice(i * PS, (i + 1) * PS)
                g_v[base + i * PS : base + (i + 1) * PS, lanes] = (
                    gx[side, rows, lanes] + te_s[side, i : i + 1, lanes] * r_s[side, rows, lanes]
                ).astype(bf16)

    with_adjoint(0)
    for load in loads[6:9]:
        load.wait()
    for copy in early + late + w_copies:
        copy.wait()
    a_copy.wait()
    with_adjoint(1)

    def product_of(chunk, row):
        return dot(w_v[chunk, pl.ds(pl.multiple_of(row, TM), TM), :], g_v[...])

    ahead = lax.rem(z + 1, 4)
    behind = lax.rem(z + 3, 4)
    far = lax.rem(z + 2, 4)

    def to_left(stage, j):
        return pltpu.make_async_remote_copy(
            src_ref=sl.at[stage, j],
            dst_ref=rl.at[stage, j],
            send_sem=rs_l.at[0, stage, j],
            recv_sem=rs_l.at[1, stage, j],
            device_id=left,
            device_id_type=MESH,
        )

    def to_right(stage, j):
        return pltpu.make_async_remote_copy(
            src_ref=sr.at[stage, j],
            dst_ref=rr.at[stage, j],
            send_sem=rs_r.at[0, stage, j],
            recv_sem=rs_r.at[1, stage, j],
            device_id=right,
            device_id_type=MESH,
        )

    def far_tiles(j, carry):
        sl[0, j] = product_of(far, j * TM).astype(bf16)
        to_left(0, j).start()
        sr[0, j] = product_of(far, 2 * TM + j * TM).astype(bf16)
        to_right(0, j).start()
        return carry

    lax.fori_loop(0, 2, far_tiles, 0)

    def direct_tiles(j, carry):
        sl[1, j] = product_of(behind, 2 * TM + j * TM).astype(bf16)
        sr[1, j] = product_of(ahead, j * TM).astype(bf16)
        return carry

    lax.fori_loop(0, 2, direct_tiles, 0)

    def follow(stage, j, before, i):
        to_left(before, i).wait_send()
        to_left(stage, j).start()
        to_right(before, i).wait_send()
        to_right(stage, j).start()

    follow(1, 0, 0, 0)

    for i in range(NH):
        rows = slice(i * PS, (i + 1) * PS)
        terms[i : i + 1, :] -= te_s[0, i : i + 1, :] * jnp.sum(
            xt[rows, :].astype(f32) * r_s[0, rows, :], axis=0, keepdims=True
        )
    from_on = (row_i >= col_i).astype(f32).astype(bf16)
    suffix = [exact_dot(terms[:, k * Q : (k + 1) * Q], from_on) for k in range(2)]
    first, second = (jnp.broadcast_to(part[:, 0:1], (NH, N)) for part in suffix)
    head_lane = (
        lax.broadcasted_iota(jnp.int32, (NH, N), 0) == lax.broadcasted_iota(jnp.int32, (NH, N), 1)
    )
    tsum[...] = jnp.sum(jnp.where(head_lane, first + second, 0.0), axis=0, keepdims=True)

    def send_sum(o, carry):
        pltpu.make_async_remote_copy(
            src_ref=tsum,
            dst_ref=rt2.at[SEQ - o],
            send_sem=a_send.at[2],
            recv_sem=a_recv.at[2],
            device_id=peer(o),
            device_id_type=MESH,
        ).start()
        return carry

    lax.fori_loop(1, SEQ, send_sum, 0)

    def next_tiles(j, carry):
        acc[0, j] = product_of(behind, j * TM)
        acc[1, j] = product_of(ahead, 2 * TM + j * TM)
        return carry

    lax.fori_loop(0, 2, next_tiles, 0)

    def own_tiles(j, carry):
        own[j] = product_of(z, j * TM)
        return carry

    lax.fori_loop(0, 4, own_tiles, 0)

    follow(1, 1, 0, 1)

    def add_later(o, total):
        return total + jnp.where(s + o < SEQ, rt2[o], 0.0)

    all_of(rt2.at[pl.ds(1, SEQ - 1)], 2).wait_recv()
    run_v[0] = lax.fori_loop(1, SEQ, add_later, jnp.zeros((1, N), f32))
    run_copy = to_sib(run_v.at[0], run_v.at[1], p_sem, 9)
    run_copy.start()

    for j in range(2):
        to_left(0, j).wait_recv()
        sl[2, j] = (acc[0, j] + rl[0, j].astype(f32)).astype(bf16)
        to_right(0, j).wait_recv()
        sr[2, j] = (acc[1, j] + rr[0, j].astype(f32)).astype(bf16)
        follow(2, j, 1, j)


    run_copy.wait()
    running = jnp.broadcast_to(run_v[1], (NH, N))
    running = jnp.sum(jnp.where(head_lane, running, 0.0), axis=1, keepdims=True)
    norm = 1.0 / math.sqrt(SEQ * TOK)
    gd_v[:, Q : 2 * Q] = (suffix[1] + running) * norm
    gd_v[:, 0:Q] = (suffix[0] + running + second[:, 0:1]) * norm

    outs = [pltpu.make_async_copy(gd_v, gd_hbm, out_sem.at[0])]
    outs[0].start()
    for j in range(2):
        to_right(1, j).wait_recv()
        to_left(2, j).wait_recv()
        a_tile = own[j] + rr[1, j].astype(f32) + rl[2, j].astype(f32)
        o_v[j * TM : (j + 1) * TM, :] = a_tile.astype(bf16)
        to_left(1, j).wait_recv()
        to_right(2, j).wait_recv()
        b_tile = own[2 + j] + rl[1, j].astype(f32) + rr[2, j].astype(f32)
        o_v[(2 + j) * TM : (3 + j) * TM, :] = b_tile.astype(bf16)
        for half in (j, 2 + j):
            rows = pl.ds(half * TM, TM)
            copy = pltpu.make_async_copy(o_v.at[rows], out_hbm.at[rows], out_sem.at[1 + half])
            copy.start()
            outs.append(copy)

    for i, ref in (
        (0, ra),
        (1, ob),
        (2, rt2.at[pl.ds(1, SEQ - 1)]),
    ):
        all_of(ref, i).wait_send()
    for j in range(2):
        to_left(2, j).wait_send()
        to_right(2, j).wait_send()
    for copy in outs:
        copy.wait()


def hand_over(out_in, decays_in, out, decays):
    out[...] = out_in[...]
    decays[...] = decays_in[...]


def body(x_in, b_proj, c_proj, decay, d_skip, block_states, grad_out, w_x, w_b, w_c):
    any_spec = pl.BlockSpec(memory_space=pl.ANY)
    dma = pltpu.SemaphoreType.DMA
    out, decays = pl.pallas_call(
        kernel,
        out_shape=(
            jax.ShapeDtypeStruct((ROWS, TOK), bf16),
            jax.ShapeDtypeStruct((NH, TOK), f32),
        ),
        in_specs=[any_spec] * 10,
        out_specs=(any_spec, any_spec),
        scratch_shapes=[
            pltpu.VMEM((TOK, HP), bf16),
            pltpu.VMEM((TOK, N), bf16),
            pltpu.VMEM((TOK, N), bf16),
            pltpu.VMEM((NH, TOK), f32),
            pltpu.VMEM((2 * HP, N), f32),
            pltpu.VMEM((TOK, HP), bf16),
            pltpu.VMEM((4, ROWS, 2 * KOWN), bf16),
            pltpu.VMEM((2 * KOWN, TOK), bf16),
            pltpu.VMEM((HP, TOK), bf16),
            pltpu.VMEM((HP, TOK), bf16),
            pltpu.VMEM((2, N, TOK), bf16),
            pltpu.VMEM((N, TOK), bf16),
            pltpu.VMEM((2, HP, TOK), bf16),
            pltpu.VMEM((HP, TOK), bf16),
            pltpu.VMEM((NH, TOK), f32),
            pltpu.VMEM((TOK, NH), f32),
            pltpu.VMEM((NH, TOK), f32),
            pltpu.VMEM((2, NH, TOK), f32),
            pltpu.VMEM((NH, N), f32),
            pltpu.VMEM((2, NH, N), f32),
            pltpu.VMEM((2, HP, N), f32),
            pltpu.VMEM((SEQ, 2 * SL, N), bf16),
            pltpu.VMEM((SEQ, 2 * SL, N), bf16),
            pltpu.VMEM((SEQ, SL, N), bf16),
            pltpu.VMEM((2, HP, N), bf16),
            pltpu.VMEM((2, HP, TOK), f32),
            pltpu.VMEM((2, N, TOK), f32),
            pltpu.VMEM((Q, Q), f32),
            pltpu.VMEM((Q, Q), f32),
            pltpu.VMEM((HP, Q), f32),
            pltpu.VMEM((2, HP, TOK), f32),
            pltpu.VMEM((NH, TOK), f32),
            pltpu.VMEM((SEQ, 1, N), f32),
            pltpu.VMEM((1, N), f32),
            pltpu.VMEM((2, 1, N), f32),
            pltpu.VMEM((3, 2, TM, TOK), bf16),
            pltpu.VMEM((3, 2, TM, TOK), bf16),
            pltpu.VMEM((3, 2, TM, TOK), bf16),
            pltpu.VMEM((3, 2, TM, TOK), bf16),
            pltpu.VMEM((4, TM, TOK), f32),
            pltpu.VMEM((2, 2, TM, TOK), f32),
            pltpu.VMEM((ROWS, TOK), bf16),
            pltpu.VMEM((NH, TOK), f32),
            pltpu.SMEM((NH,), f32),
            dma((10,)),
            dma((2, 3)),
            dma((2, 10)),
            dma((3,)),
            dma((3,)),
            dma((2, 3, 2)),
            dma((2, 3, 2)),
            dma((5,)),
        ],
        compiler_params=pltpu.CompilerParams(
            collective_id=0, has_side_effects=True, vmem_limit_bytes=60 * 2**20
        ),
    )(
        x_in,
        b_proj,
        c_proj,
        decay,
        d_skip,
        block_states.reshape(2 * HP, N),
        grad_out,
        w_x.reshape(4, 2, ROWS, HP),
        w_b.reshape(4, 2, ROWS, N),
        w_c.reshape(4, 2, ROWS, N),
    )
    return pl.pallas_call(
        hand_over,
        out_shape=(
            jax.ShapeDtypeStruct((ROWS, TOK), bf16),
            jax.ShapeDtypeStruct((NH, TOK), f32),
        ),
    )(out, decays)


def solution(mesh):
    return jax.shard_map(
        body,
        mesh=mesh,
        in_specs=(
            P("seq", "head"),
            P("seq", "head"),
            P("seq", "head"),
            P("head", "seq"),
            P("head"),
            P("seq", "head", None, None),
            P("seq", "head"),
            P(None, "head"),
            P(None, "head"),
            P(None, "head"),
        ),
        out_specs=(P("head", "seq"), P("head", "seq")),
        check_vma=False,
    )
```

```python
import math

import jax
import jax.numpy as jnp
from jax import lax
from jax.experimental import pallas as pl
from jax.experimental.pallas import tpu as pltpu
from jax.sharding import PartitionSpec as P

SEQ = 32
HEAD = 8
TOK = 512
Q = 256
NH = 8
PS = 64
N = 128
HP = NH * PS
KOWN = HP + 2 * N
ROWS = 512
TM = 128
SL = HP // SEQ

NZ, NX, NY = 2, 4, 4
STEPS = sorted(
    ((a, b, c) for a in range(NZ) for b in range(NX) for c in range(NY)),
    key=lambda t: -(min(t[0], NZ - t[0]) + min(t[1], NX - t[1]) + min(t[2], NY - t[2])),
)

MESH = pl.DeviceIdType.MESH
f32 = jnp.float32
bf16 = jnp.bfloat16

TN = (((0,), (0,)), ((), ()))
NT = (((1,), (1,)), ((), ()))


def dot(a, b, dims=(((1,), (0,)), ((), ()))):
    return lax.dot_general(a, b, dims, preferred_element_type=f32)


def split3(v):
    hi = v.astype(bf16).astype(f32)
    rest = v - hi
    mid = rest.astype(bf16).astype(f32)
    low = rest - mid
    return jnp.concatenate([hi, mid, low], axis=0).astype(bf16)


def exact_dot(v, mask):
    rows = v.shape[0]
    out = dot(split3(v), mask)
    return out[0:rows] + out[rows : 2 * rows] + out[2 * rows : 3 * rows]


def kernel(
    x_hbm, b_hbm, c_hbm, dec_hbm, skip_hbm, st_hbm, dy_hbm, wx_hbm, wb_hbm, wc_hbm,
    out_hbm, gd_hbm,
    x_v, b_v, c_v, dec_v, st_v, dy_v, w_v, g_v,
    xt, dyt, bt, ct, xte, dyfs, cum_s, cumt_s, fs_s, te_s, th0, th1,
    adj1, msg, ra, ob, a_v,
    gx, gb, wd, cb, yi, r_s, terms, rt2, tsum, run_v,
    sl, rl, sr, rr, own, acc, o_v, gd_v, skip_ref,
    load_sem, w_sem, p_sem, a_send, a_recv, rs_l, rs_r, out_sem,
):
    s = lax.axis_index("seq")
    h = lax.axis_index("head")
    z = h // 2
    core = lax.rem(h, 2)
    sib = (s, h + 1 - 2 * core)
    left = (s, lax.rem(h + HEAD - 2, HEAD))
    right = (s, lax.rem(h + 2, HEAD))

    at_z, at_x, at_y = s // (NX * NY), lax.rem(s // NY, NX), lax.rem(s, NY)

    def peer_at(step):
        return (
            lax.rem(at_z + step[0], NZ) * (NX * NY)
            + lax.rem(at_x + step[1], NX) * NY
            + lax.rem(at_y + step[2], NY)
        )

    def slot_at(step):
        a, b, c = ((size - i) % size for size, i in zip((NZ, NX, NY), step))
        return (a * NX + b) * NY + c

    def slot_of(d):
        return (
            lax.rem(d // (NX * NY) - at_z + NZ, NZ) * (NX * NY)
            + lax.rem(lax.rem(d // NY, NX) - at_x + NX, NX) * NY
            + lax.rem(lax.rem(d, NY) - at_y + NY, NY)
        )

    barrier = pltpu.get_barrier_semaphore()

    for step in STEPS:
        other = (peer_at(step), sib[1])
        pl.semaphore_signal(barrier, inc=1, device_id=other, device_id_type=MESH)
        if any(step):
            other = (peer_at(step), h)
            pl.semaphore_signal(barrier, inc=1, device_id=other, device_id_type=MESH)
    for other in (left, right):
        pl.semaphore_signal(barrier, inc=1, device_id=other, device_id_type=MESH)

    loads = [
        pltpu.make_async_copy(src, dst, load_sem.at[i])
        for i, (src, dst) in enumerate(
            (
                (dec_hbm, dec_v),
                (dy_hbm, dy_v),
                (c_hbm, c_v),
                (b_hbm, b_v),
                (x_hbm, x_v),
                (st_hbm, st_v),
                (wx_hbm.at[:, core], w_v.at[:, :, 0:HP]),
                (wb_hbm.at[:, core], w_v.at[:, :, HP : HP + N]),
                (wc_hbm.at[:, core], w_v.at[:, :, HP + N : KOWN]),
                (skip_hbm, skip_ref),
            )
        )
    ]
    for load in loads:
        load.start()

    row_i = lax.broadcasted_iota(jnp.int32, (Q, Q), 0)
    col_i = lax.broadcasted_iota(jnp.int32, (Q, Q), 1)

    loads[0].wait()
    upto = (row_i <= col_i).astype(f32).astype(bf16)
    log_decay = jnp.log(dec_v[...])
    for k in range(2):
        lanes = slice(k * Q, (k + 1) * Q)
        cum = exact_dot(log_decay[:, lanes], upto)
        cum_s[:, lanes] = cum
        fs_s[:, lanes] = jnp.exp(cum)
        last = jnp.broadcast_to(cum[:, Q - 1 : Q], (NH, Q))
        te_s[0, :, lanes] = jnp.exp(last - cum)
        (th0, th1.at[0])[k][...] = jnp.exp(last[:, 0:N])
    through = th0[...] * th1[0]
    coarse = through.astype(bf16).astype(f32)
    fine = through - coarse
    factors = [
        jnp.concatenate(
            [jnp.broadcast_to(part[i : i + 1, :], (SL // 2, N)) for part in (coarse, fine)], axis=0
        ).astype(bf16)
        for i in range(NH)
    ]

    loads[1].wait()
    dyt[...] = dy_v[...].T
    for i in range(NH):
        rows = slice(i * PS, (i + 1) * PS)
        dyfs[rows, :] = (dyt[rows, :].astype(f32) * fs_s[i : i + 1, :]).astype(bf16)
    loads[2].wait()
    adj1[0] = dot(dyfs[:, Q : 2 * Q], c_v[Q : 2 * Q, :])
    adj0 = dot(dyfs[:, 0:Q], c_v[0:Q, :])
    for i in range(SEQ):
        rows = slice(i * SL, (i + 1) * SL)
        head = i * SL // PS
        msg[i, 0:SL] = (adj0[rows, :] + th0[head : head + 1, :] * adj1[0, rows, :]).astype(bf16)
        msg[i, SL : 2 * SL] = factors[head]

    pl.semaphore_wait(barrier, 2 * SEQ + 1)

    for step in STEPS:
        to = peer_at(step)
        pltpu.make_async_remote_copy(
            src_ref=msg.at[to],
            dst_ref=ra.at[slot_at(step)],
            send_sem=a_send.at[0],
            recv_sem=a_recv.at[0],
            device_id=(to, sib[1]),
            device_id_type=MESH,
        ).start()

    def to_sib(src, dst, sems, i):
        return pltpu.make_async_remote_copy(
            src_ref=src,
            dst_ref=dst,
            send_sem=sems.at[0, i],
            recv_sem=sems.at[1, i],
            device_id=sib,
            device_id_type=MESH,
        )

    w_copies = [
        to_sib(src.at[:, 1 - core], w_v.at[:, :, lo:hi], w_sem, i)
        for i, (src, lo, hi) in enumerate(
            (
                (wx_hbm, KOWN, KOWN + HP),
                (wb_hbm, KOWN + HP, KOWN + HP + N),
                (wc_hbm, KOWN + HP + N, 2 * KOWN),
            )
        )
    ]
    early = [
        to_sib(ref.at[0], ref.at[1], p_sem, i) for i, ref in enumerate((te_s, th1, adj1, bt, xte))
    ]
    for copy in w_copies:
        copy.start()

    loads[4].wait()
    xt[...] = x_v[...].T
    for i in range(NH):
        rows = slice(i * PS, (i + 1) * PS)
        xte[0, rows, :] = (xt[rows, :].astype(f32) * te_s[0, i : i + 1, :]).astype(bf16)
    loads[3].wait()
    bt[0] = b_v[...].T
    ct[...] = c_v[...].T
    cumt_s[...] = cum_s[...].T

    loads[5].wait()
    loads[9].wait()
    def block(k, carry):
        lanes = pl.ds(pl.multiple_of(k * Q, Q), Q)
        srows = pl.ds(pl.multiple_of(k * HP, HP), HP)
        c_k = c_v[lanes, :]
        bt_k = bt[0, :, lanes]
        ct_k = ct[:, lanes]
        s0 = st_v[srows, :].astype(bf16)
        cb[...] = dot(c_k, bt_k)
        yi[...] = dot(s0, ct_k)
        causal = row_i >= col_i
        for i in range(NH):
            rows = slice(i * PS, (i + 1) * PS)
            xh = xt[rows, lanes]
            dyh = dyt[rows, lanes]
            gaps = cumt_s[lanes, i : i + 1] - cum_s[i : i + 1, lanes]
            decay = jnp.exp(jnp.where(causal, gaps, -1e30))
            forward = (decay * cb[...]).astype(bf16)
            product = dot(dy_v[lanes, rows], xh)
            if i == 0:
                wd[...] = decay * product
            else:
                wd[...] += decay * product
            gx0 = dot(dyh, forward)
            y = dot(xh, forward, NT) + fs_s[i : i + 1, lanes] * yi[rows, :]
            dyf = dyh.astype(f32)
            terms[i : i + 1, lanes] = jnp.sum(dyf * y - xh.astype(f32) * gx0, axis=0, keepdims=True)
            gx[0, rows, lanes] = gx0 + skip_ref[i] * dyf
        decayed = wd[...].astype(bf16)
        gb[0, :, lanes] = dot(ct_k, decayed)
        gc = dot(bt_k, decayed, NT) + dot(s0, dyfs[:, lanes], TN)
        g_v[HP + N : KOWN, lanes] = gc.astype(bf16)
        return carry

    for copy in early:
        copy.start()
    lax.fori_loop(0, 2, block, 0)

    late = [
        to_sib(src, dst, p_sem, 5 + i)
        for i, (src, dst) in enumerate(
            (
                (gx.at[0], gx.at[1]),
                (gb.at[0], gb.at[1]),
                (g_v.at[pl.ds(HP + N, N)], g_v.at[pl.ds(KOWN + HP + N, N)]),
            )
        )
    ]
    for copy in late:
        copy.start()

    def all_of(ref, i):
        return pltpu.make_async_remote_copy(
            src_ref=ref,
            dst_ref=ref,
            send_sem=a_send.at[i],
            recv_sem=a_recv.at[i],
            device_id=sib,
            device_id_type=MESH,
        )

    all_of(ra, 0).wait_recv()

    def scan(step, cur):
        d = SEQ - 1 - step
        slot = slot_of(d)
        ob[d] = cur.astype(bf16)
        parts = ra[slot, SL : 2 * SL, :].astype(f32)
        factor = parts[0 : SL // 2, :] + parts[SL // 2 : SL, :]
        return ra[slot, 0:SL, :].astype(f32) + jnp.concatenate([factor, factor], axis=0) * cur

    cur = jnp.zeros((SL, N), f32)
    for step in range(SEQ):
        cur = scan(step, cur)
    own_rows = pl.ds(pl.multiple_of(s * SL, SL), SL)

    a_v[1, own_rows, :] = ob[s]
    for step in STEPS:
        to = peer_at(step)
        pltpu.make_async_remote_copy(
            src_ref=ob.at[to],
            dst_ref=a_v.at[0, own_rows],
            send_sem=a_send.at[1],
            recv_sem=a_recv.at[1],
            device_id=(to, sib[1]),
            device_id_type=MESH,
        ).start()
        if any(step):
            pltpu.make_async_remote_copy(
                src_ref=ob.at[to],
                dst_ref=a_v.at[1, own_rows],
                send_sem=a_send.at[3],
                recv_sem=a_recv.at[3],
                device_id=(to, h),
                device_id_type=MESH,
            ).start()

    all_of(a_v.at[0], 1).wait_recv()

    def with_adjoint(side):
        for k in (1, 0):
            lanes = slice(k * Q, (k + 1) * Q)
            later = a_v[side]
            if k == 0:
                later = jnp.concatenate(
                    [
                        (
                            adj1[side, i * PS : (i + 1) * PS, :]
                            + th1[side, i : i + 1, :]
                            * a_v[side, i * PS : (i + 1) * PS, :].astype(f32)
                        ).astype(bf16)
                        for i in range(NH)
                    ],
                    axis=0,
                )
            r_s[side, :, lanes] = dot(later, bt[side, :, lanes])
            base = side * KOWN
            g_v[base + HP : base + HP + N, lanes] = (
                gb[side, :, lanes] + dot(later, xte[side, :, lanes], TN)
            ).astype(bf16)
            for i in range(NH):
                rows = slice(i * PS, (i + 1) * PS)
                g_v[base + i * PS : base + (i + 1) * PS, lanes] = (
                    gx[side, rows, lanes] + te_s[side, i : i + 1, lanes] * r_s[side, rows, lanes]
                ).astype(bf16)

    with_adjoint(0)
    for load in loads[6:9]:
        load.wait()
    for copy in early + late + w_copies:
        copy.wait()
    all_of(a_v.at[1, pl.ds(0, HP - SL)], 3).wait_recv()
    with_adjoint(1)

    def product_of(chunk, row):
        return dot(w_v[chunk, pl.ds(pl.multiple_of(row, TM), TM), :], g_v[...])

    ahead = lax.rem(z + 1, 4)
    behind = lax.rem(z + 3, 4)
    far = lax.rem(z + 2, 4)

    def to_left(stage, j):
        return pltpu.make_async_remote_copy(
            src_ref=sl.at[stage, j],
            dst_ref=rl.at[stage, j],
            send_sem=rs_l.at[0, stage, j],
            recv_sem=rs_l.at[1, stage, j],
            device_id=left,
            device_id_type=MESH,
        )

    def to_right(stage, j):
        return pltpu.make_async_remote_copy(
            src_ref=sr.at[stage, j],
            dst_ref=rr.at[stage, j],
            send_sem=rs_r.at[0, stage, j],
            recv_sem=rs_r.at[1, stage, j],
            device_id=right,
            device_id_type=MESH,
        )

    def far_tiles(j, carry):
        sl[0, j] = product_of(far, j * TM).astype(bf16)
        to_left(0, j).start()
        sr[0, j] = product_of(far, 2 * TM + j * TM).astype(bf16)
        to_right(0, j).start()
        return carry

    lax.fori_loop(0, 2, far_tiles, 0)

    def direct_tiles(j, carry):
        sl[1, j] = product_of(behind, 2 * TM + j * TM).astype(bf16)
        sr[1, j] = product_of(ahead, j * TM).astype(bf16)
        return carry

    lax.fori_loop(0, 2, direct_tiles, 0)

    def follow(stage, j, before, i):
        to_left(before, i).wait_send()
        to_left(stage, j).start()
        to_right(before, i).wait_send()
        to_right(stage, j).start()

    follow(1, 0, 0, 0)

    for i in range(NH):
        rows = slice(i * PS, (i + 1) * PS)
        terms[i : i + 1, :] -= te_s[0, i : i + 1, :] * jnp.sum(
            xt[rows, :].astype(f32) * r_s[0, rows, :], axis=0, keepdims=True
        )
    from_on = (row_i >= col_i).astype(f32).astype(bf16)
    suffix = [exact_dot(terms[:, k * Q : (k + 1) * Q], from_on) for k in range(2)]
    first, second = (jnp.broadcast_to(part[:, 0:1], (NH, N)) for part in suffix)
    head_lane = (
        lax.broadcasted_iota(jnp.int32, (NH, N), 0) == lax.broadcasted_iota(jnp.int32, (NH, N), 1)
    )
    tsum[...] = jnp.sum(jnp.where(head_lane, first + second, 0.0), axis=0, keepdims=True)

    def send_sum(o, carry):
        pltpu.make_async_remote_copy(
            src_ref=tsum,
            dst_ref=rt2.at[SEQ - o],
            send_sem=a_send.at[2],
            recv_sem=a_recv.at[2],
            device_id=(lax.rem(s + o, SEQ), sib[1]),
            device_id_type=MESH,
        ).start()
        return carry

    lax.fori_loop(1, SEQ, send_sum, 0)

    def next_tiles(j, carry):
        acc[0, j] = product_of(behind, j * TM)
        acc[1, j] = product_of(ahead, 2 * TM + j * TM)
        return carry

    lax.fori_loop(0, 2, next_tiles, 0)

    def own_tiles(j, carry):
        own[j] = product_of(z, j * TM)
        return carry

    lax.fori_loop(0, 4, own_tiles, 0)

    follow(1, 1, 0, 1)

    def add_later(o, total):
        return total + jnp.where(s + o < SEQ, rt2[o], 0.0)

    all_of(rt2.at[pl.ds(1, SEQ - 1)], 2).wait_recv()
    run_v[0] = lax.fori_loop(1, SEQ, add_later, jnp.zeros((1, N), f32))
    run_copy = to_sib(run_v.at[0], run_v.at[1], p_sem, 8)
    run_copy.start()

    for j in range(2):
        to_left(0, j).wait_recv()
        sl[2, j] = (acc[0, j] + rl[0, j].astype(f32)).astype(bf16)
        to_right(0, j).wait_recv()
        sr[2, j] = (acc[1, j] + rr[0, j].astype(f32)).astype(bf16)
        follow(2, j, 1, j)


    run_copy.wait()
    running = jnp.broadcast_to(run_v[1], (NH, N))
    running = jnp.sum(jnp.where(head_lane, running, 0.0), axis=1, keepdims=True)
    norm = 1.0 / math.sqrt(SEQ * TOK)
    gd_v[:, Q : 2 * Q] = (suffix[1] + running) * norm
    gd_v[:, 0:Q] = (suffix[0] + running + second[:, 0:1]) * norm

    outs = [pltpu.make_async_copy(gd_v, gd_hbm, out_sem.at[0])]
    outs[0].start()
    for j in range(2):
        to_right(1, j).wait_recv()
        to_left(2, j).wait_recv()
        a_tile = own[j] + rr[1, j].astype(f32) + rl[2, j].astype(f32)
        o_v[j * TM : (j + 1) * TM, :] = a_tile.astype(bf16)
        to_left(1, j).wait_recv()
        to_right(2, j).wait_recv()
        b_tile = own[2 + j] + rl[1, j].astype(f32) + rr[2, j].astype(f32)
        o_v[(2 + j) * TM : (3 + j) * TM, :] = b_tile.astype(bf16)
        for half in (j, 2 + j):
            rows = pl.ds(half * TM, TM)
            copy = pltpu.make_async_copy(o_v.at[rows], out_hbm.at[rows], out_sem.at[1 + half])
            copy.start()
            outs.append(copy)

    for i, ref in (
        (0, ra),
        (1, ob),
        (3, ob.at[pl.ds(1, SEQ - 1)]),
        (2, rt2.at[pl.ds(1, SEQ - 1)]),
    ):
        all_of(ref, i).wait_send()
    for j in range(2):
        to_left(2, j).wait_send()
        to_right(2, j).wait_send()
    for copy in outs:
        copy.wait()


def hand_over(out_in, decays_in, out, decays):
    out[...] = out_in[...]
    decays[...] = decays_in[...]


def body(x_in, b_proj, c_proj, decay, d_skip, block_states, grad_out, w_x, w_b, w_c):
    any_spec = pl.BlockSpec(memory_space=pl.ANY)
    dma = pltpu.SemaphoreType.DMA
    out, decays = pl.pallas_call(
        kernel,
        out_shape=(
            jax.ShapeDtypeStruct((ROWS, TOK), bf16),
            jax.ShapeDtypeStruct((NH, TOK), f32),
        ),
        in_specs=[any_spec] * 10,
        out_specs=(any_spec, any_spec),
        scratch_shapes=[
            pltpu.VMEM((TOK, HP), bf16),
            pltpu.VMEM((TOK, N), bf16),
            pltpu.VMEM((TOK, N), bf16),
            pltpu.VMEM((NH, TOK), f32),
            pltpu.VMEM((2 * HP, N), f32),
            pltpu.VMEM((TOK, HP), bf16),
            pltpu.VMEM((4, ROWS, 2 * KOWN), bf16),
            pltpu.VMEM((2 * KOWN, TOK), bf16),
            pltpu.VMEM((HP, TOK), bf16),
            pltpu.VMEM((HP, TOK), bf16),
            pltpu.VMEM((2, N, TOK), bf16),
            pltpu.VMEM((N, TOK), bf16),
            pltpu.VMEM((2, HP, TOK), bf16),
            pltpu.VMEM((HP, TOK), bf16),
            pltpu.VMEM((NH, TOK), f32),
            pltpu.VMEM((TOK, NH), f32),
            pltpu.VMEM((NH, TOK), f32),
            pltpu.VMEM((2, NH, TOK), f32),
            pltpu.VMEM((NH, N), f32),
            pltpu.VMEM((2, NH, N), f32),
            pltpu.VMEM((2, HP, N), f32),
            pltpu.VMEM((SEQ, 2 * SL, N), bf16),
            pltpu.VMEM((SEQ, 2 * SL, N), bf16),
            pltpu.VMEM((SEQ, SL, N), bf16),
            pltpu.VMEM((2, HP, N), bf16),
            pltpu.VMEM((2, HP, TOK), f32),
            pltpu.VMEM((2, N, TOK), f32),
            pltpu.VMEM((Q, Q), f32),
            pltpu.VMEM((Q, Q), f32),
            pltpu.VMEM((HP, Q), f32),
            pltpu.VMEM((2, HP, TOK), f32),
            pltpu.VMEM((NH, TOK), f32),
            pltpu.VMEM((SEQ, 1, N), f32),
            pltpu.VMEM((1, N), f32),
            pltpu.VMEM((2, 1, N), f32),
            pltpu.VMEM((3, 2, TM, TOK), bf16),
            pltpu.VMEM((3, 2, TM, TOK), bf16),
            pltpu.VMEM((3, 2, TM, TOK), bf16),
            pltpu.VMEM((3, 2, TM, TOK), bf16),
            pltpu.VMEM((4, TM, TOK), f32),
            pltpu.VMEM((2, 2, TM, TOK), f32),
            pltpu.VMEM((ROWS, TOK), bf16),
            pltpu.VMEM((NH, TOK), f32),
            pltpu.SMEM((NH,), f32),
            dma((10,)),
            dma((2, 3)),
            dma((2, 9)),
            dma((4,)),
            dma((4,)),
            dma((2, 3, 2)),
            dma((2, 3, 2)),
            dma((5,)),
        ],
        compiler_params=pltpu.CompilerParams(
            collective_id=0, has_side_effects=True, vmem_limit_bytes=60 * 2**20
        ),
    )(
        x_in,
        b_proj,
        c_proj,
        decay,
        d_skip,
        block_states.reshape(2 * HP, N),
        grad_out,
        w_x.reshape(4, 2, ROWS, HP),
        w_b.reshape(4, 2, ROWS, N),
        w_c.reshape(4, 2, ROWS, N),
    )
    return pl.pallas_call(
        hand_over,
        out_shape=(
            jax.ShapeDtypeStruct((ROWS, TOK), bf16),
            jax.ShapeDtypeStruct((NH, TOK), f32),
        ),
    )(out, decays)


def solution(mesh):
    return jax.shard_map(
        body,
        mesh=mesh,
        in_specs=(
            P("seq", "head"),
            P("seq", "head"),
            P("seq", "head"),
            P("head", "seq"),
            P("head"),
            P("seq", "head", None, None),
            P("seq", "head"),
            P(None, "head"),
            P(None, "head"),
            P(None, "head"),
        ),
        out_specs=(P("head", "seq"), P("head", "seq")),
        check_vma=False,
    )
```

```python
import math

import jax
import jax.numpy as jnp
from jax import lax
from jax.experimental import pallas as pl
from jax.experimental.pallas import tpu as pltpu
from jax.sharding import PartitionSpec as P

SEQ = 32
HEAD = 8
TOK = 512
Q = 256
NH = 8
PS = 64
N = 128
HP = NH * PS
KOWN = HP + 2 * N
ROWS = 512
TM = 128
SL = HP // SEQ

NZ, NX, NY = 2, 4, 4
STEPS = sorted(
    ((a, b, c) for a in range(NZ) for b in range(NX) for c in range(NY)),
    key=lambda t: -(min(t[0], NZ - t[0]) + min(t[1], NX - t[1]) + min(t[2], NY - t[2])),
)

MESH = pl.DeviceIdType.MESH
f32 = jnp.float32
bf16 = jnp.bfloat16

TN = (((0,), (0,)), ((), ()))
NT = (((1,), (1,)), ((), ()))


def dot(a, b, dims=(((1,), (0,)), ((), ()))):
    return lax.dot_general(a, b, dims, preferred_element_type=f32)


def split3(v):
    hi = v.astype(bf16).astype(f32)
    rest = v - hi
    mid = rest.astype(bf16).astype(f32)
    low = rest - mid
    return jnp.concatenate([hi, mid, low], axis=0).astype(bf16)


def exact_dot(v, mask):
    rows = v.shape[0]
    out = dot(split3(v), mask)
    return out[0:rows] + out[rows : 2 * rows] + out[2 * rows : 3 * rows]


def kernel(
    x_hbm, b_hbm, c_hbm, dec_hbm, skip_hbm, st_hbm, dy_hbm, wx_hbm, wb_hbm, wc_hbm,
    out_hbm, last_hbm, gd_hbm,
    x_v, b_v, c_v, dec_v, st_v, dy_v, w_v, g_v,
    xt, dyt, bt, ct, xte, dyfs, cum_s, cumt_s, fs_s, te_s, th0, th1,
    adj1, msg, ra, tt_s, rt, ob, a_v,
    gx, gb, wd, cb, yi, r_s, terms, rt2, tsum, run_v,
    sl, rl, sr, rr, own, acc, o_v, gd_v, skip_ref,
    load_sem, w_sem, p_sem, a_send, a_recv, rs_l, rs_r, out_sem,
):
    s = lax.axis_index("seq")
    h = lax.axis_index("head")
    z = h // 2
    core = lax.rem(h, 2)
    sib = (s, h + 1 - 2 * core)
    left = (s, lax.rem(h + HEAD - 2, HEAD))
    right = (s, lax.rem(h + 2, HEAD))

    at_z, at_x, at_y = s // (NX * NY), lax.rem(s // NY, NX), lax.rem(s, NY)

    def peer_at(step):
        return (
            lax.rem(at_z + step[0], NZ) * (NX * NY)
            + lax.rem(at_x + step[1], NX) * NY
            + lax.rem(at_y + step[2], NY)
        )

    def slot_at(step):
        a, b, c = ((size - i) % size for size, i in zip((NZ, NX, NY), step))
        return (a * NX + b) * NY + c

    def slot_of(d):
        return (
            lax.rem(d // (NX * NY) - at_z + NZ, NZ) * (NX * NY)
            + lax.rem(lax.rem(d // NY, NX) - at_x + NX, NX) * NY
            + lax.rem(lax.rem(d, NY) - at_y + NY, NY)
        )

    barrier = pltpu.get_barrier_semaphore()

    for step in STEPS:
        other = (peer_at(step), sib[1])
        pl.semaphore_signal(barrier, inc=1, device_id=other, device_id_type=MESH)
        if any(step):
            other = (peer_at(step), h)
            pl.semaphore_signal(barrier, inc=1, device_id=other, device_id_type=MESH)
    for other in (left, right):
        pl.semaphore_signal(barrier, inc=1, device_id=other, device_id_type=MESH)

    loads = [
        pltpu.make_async_copy(src, dst, load_sem.at[i])
        for i, (src, dst) in enumerate(
            (
                (dec_hbm, dec_v),
                (dy_hbm, dy_v),
                (c_hbm, c_v),
                (b_hbm, b_v),
                (x_hbm, x_v),
                (st_hbm, st_v),
                (wx_hbm.at[:, core], w_v.at[:, :, 0:HP]),
                (wb_hbm.at[:, core], w_v.at[:, :, HP : HP + N]),
                (wc_hbm.at[:, core], w_v.at[:, :, HP + N : KOWN]),
                (skip_hbm, skip_ref),
            )
        )
    ]
    for load in loads:
        load.start()

    row_i = lax.broadcasted_iota(jnp.int32, (Q, Q), 0)
    col_i = lax.broadcasted_iota(jnp.int32, (Q, Q), 1)

    loads[0].wait()
    upto = (row_i <= col_i).astype(f32).astype(bf16)
    log_decay = jnp.log(dec_v[...])
    for k in range(2):
        lanes = slice(k * Q, (k + 1) * Q)
        cum = exact_dot(log_decay[:, lanes], upto)
        cum_s[:, lanes] = cum
        fs_s[:, lanes] = jnp.exp(cum)
        last = jnp.broadcast_to(cum[:, Q - 1 : Q], (NH, Q))
        te_s[0, :, lanes] = jnp.exp(last - cum)
        (th0, th1.at[0])[k][...] = jnp.exp(last[:, 0:N])
    through = th0[...] * th1[0]
    for i in range(NH):
        tt_s[i] = through[i : i + 1, :]

    loads[1].wait()
    dyt[...] = dy_v[...].T
    for i in range(NH):
        rows = slice(i * PS, (i + 1) * PS)
        dyfs[rows, :] = (dyt[rows, :].astype(f32) * fs_s[i : i + 1, :]).astype(bf16)
    loads[2].wait()
    adj1[0] = dot(dyfs[:, Q : 2 * Q], c_v[Q : 2 * Q, :])
    adj0 = dot(dyfs[:, 0:Q], c_v[0:Q, :])
    for i in range(SEQ):
        rows = slice(i * SL, (i + 1) * SL)
        head = i * SL // PS
        msg[i] = (adj0[rows, :] + th0[head : head + 1, :] * adj1[0, rows, :]).astype(bf16)

    pl.semaphore_wait(barrier, 2 * SEQ + 1)

    for step in STEPS:
        to = peer_at(step)
        pltpu.make_async_remote_copy(
            src_ref=msg.at[to],
            dst_ref=ra.at[slot_at(step)],
            send_sem=a_send.at[0],
            recv_sem=a_recv.at[0],
            device_id=(to, sib[1]),
            device_id_type=MESH,
        ).start()
        pltpu.make_async_remote_copy(
            src_ref=tt_s.at[to // (SEQ // NH)],
            dst_ref=rt.at[slot_at(step)],
            send_sem=a_send.at[4],
            recv_sem=a_recv.at[4],
            device_id=(to, sib[1]),
            device_id_type=MESH,
        ).start()

    def to_sib(src, dst, sems, i):
        return pltpu.make_async_remote_copy(
            src_ref=src,
            dst_ref=dst,
            send_sem=sems.at[0, i],
            recv_sem=sems.at[1, i],
            device_id=sib,
            device_id_type=MESH,
        )

    w_copies = [
        to_sib(src.at[:, 1 - core], w_v.at[:, :, lo:hi], w_sem, i)
        for i, (src, lo, hi) in enumerate(
            (
                (wx_hbm, KOWN, KOWN + HP),
                (wb_hbm, KOWN + HP, KOWN + HP + N),
                (wc_hbm, KOWN + HP + N, 2 * KOWN),
            )
        )
    ]
    early = [
        to_sib(ref.at[0], ref.at[1], p_sem, i) for i, ref in enumerate((te_s, th1, adj1, bt, xte))
    ]
    for copy in w_copies:
        copy.start()

    loads[4].wait()
    xt[...] = x_v[...].T
    for i in range(NH):
        rows = slice(i * PS, (i + 1) * PS)
        xte[0, rows, :] = (xt[rows, :].astype(f32) * te_s[0, i : i + 1, :]).astype(bf16)
    loads[3].wait()
    bt[0] = b_v[...].T
    ct[...] = c_v[...].T
    cumt_s[...] = cum_s[...].T

    loads[5].wait()
    loads[9].wait()
    def block(k, carry):
        lanes = pl.ds(pl.multiple_of(k * Q, Q), Q)
        srows = pl.ds(pl.multiple_of(k * HP, HP), HP)
        c_k = c_v[lanes, :]
        bt_k = bt[0, :, lanes]
        ct_k = ct[:, lanes]
        s0 = st_v[srows, :].astype(bf16)
        cb[...] = dot(c_k, bt_k)
        yi[...] = dot(s0, ct_k)
        causal = row_i >= col_i
        for i in range(NH):
            rows = slice(i * PS, (i + 1) * PS)
            xh = xt[rows, lanes]
            dyh = dyt[rows, lanes]
            gaps = cumt_s[lanes, i : i + 1] - cum_s[i : i + 1, lanes]
            decay = jnp.exp(jnp.where(causal, gaps, -1e30))
            forward = (decay * cb[...]).astype(bf16)
            product = dot(dy_v[lanes, rows], xh)
            if i == 0:
                wd[...] = decay * product
            else:
                wd[...] += decay * product
            gx0 = dot(dyh, forward)
            y = dot(xh, forward, NT) + fs_s[i : i + 1, lanes] * yi[rows, :]
            dyf = dyh.astype(f32)
            terms[i : i + 1, lanes] = jnp.sum(dyf * y - xh.astype(f32) * gx0, axis=0, keepdims=True)
            gx[0, rows, lanes] = gx0 + skip_ref[i] * dyf
        decayed = wd[...].astype(bf16)
        gb[0, :, lanes] = dot(ct_k, decayed)
        gc = dot(bt_k, decayed, NT) + dot(s0, dyfs[:, lanes], TN)
        g_v[HP + N : KOWN, lanes] = gc.astype(bf16)
        return carry

    for copy in early:
        copy.start()
    lax.fori_loop(0, 2, block, 0)

    late = [
        to_sib(src, dst, p_sem, 5 + i)
        for i, (src, dst) in enumerate(
            (
                (gx.at[0], gx.at[1]),
                (gb.at[0], gb.at[1]),
                (g_v.at[pl.ds(HP + N, N)], g_v.at[pl.ds(KOWN + HP + N, N)]),
            )
        )
    ]
    for copy in late:
        copy.start()

    def all_of(ref, i):
        return pltpu.make_async_remote_copy(
            src_ref=ref,
            dst_ref=ref,
            send_sem=a_send.at[i],
            recv_sem=a_recv.at[i],
            device_id=sib,
            device_id_type=MESH,
        )

    all_of(ra, 0).wait_recv()
    all_of(rt, 4).wait_recv()

    def scan(step, cur):
        d = SEQ - 1 - step
        slot = slot_of(d)
        ob[d] = cur.astype(bf16)
        return ra[slot].astype(f32) + rt[slot] * cur

    cur = jnp.zeros((SL, N), f32)
    for step in range(SEQ):
        cur = scan(step, cur)
    own_rows = pl.ds(pl.multiple_of(s * SL, SL), SL)

    a_v[1, own_rows, :] = ob[s]
    for step in STEPS:
        to = peer_at(step)
        pltpu.make_async_remote_copy(
            src_ref=ob.at[to],
            dst_ref=a_v.at[0, own_rows],
            send_sem=a_send.at[1],
            recv_sem=a_recv.at[1],
            device_id=(to, sib[1]),
            device_id_type=MESH,
        ).start()
        if any(step):
            pltpu.make_async_remote_copy(
                src_ref=ob.at[to],
                dst_ref=a_v.at[1, own_rows],
                send_sem=a_send.at[3],
                recv_sem=a_recv.at[3],
                device_id=(to, h),
                device_id_type=MESH,
            ).start()

    all_of(a_v.at[0], 1).wait_recv()

    def with_adjoint(side):
        for k in (1, 0):
            lanes = slice(k * Q, (k + 1) * Q)
            later = a_v[side]
            if k == 0:
                later = jnp.concatenate(
                    [
                        (
                            adj1[side, i * PS : (i + 1) * PS, :]
                            + th1[side, i : i + 1, :]
                            * a_v[side, i * PS : (i + 1) * PS, :].astype(f32)
                        ).astype(bf16)
                        for i in range(NH)
                    ],
                    axis=0,
                )
            r_s[side, :, lanes] = dot(later, bt[side, :, lanes])
            base = side * KOWN
            g_v[base + HP : base + HP + N, lanes] = (
                gb[side, :, lanes] + dot(later, xte[side, :, lanes], TN)
            ).astype(bf16)
            for i in range(NH):
                rows = slice(i * PS, (i + 1) * PS)
                g_v[base + i * PS : base + (i + 1) * PS, lanes] = (
                    gx[side, rows, lanes] + te_s[side, i : i + 1, lanes] * r_s[side, rows, lanes]
                ).astype(bf16)

    with_adjoint(0)
    for load in loads[6:9]:
        load.wait()
    for copy in early + late + w_copies:
        copy.wait()
    all_of(a_v.at[1, pl.ds(0, HP - SL)], 3).wait_recv()
    with_adjoint(1)

    def product_of(chunk, row):
        return dot(w_v[chunk, pl.ds(pl.multiple_of(row, TM), TM), :], g_v[...])

    ahead = lax.rem(z + 1, 4)
    behind = lax.rem(z + 3, 4)
    far = lax.rem(z + 2, 4)

    def to_left(stage, j):
        landing = last_hbm.at[pl.ds(j * TM, TM)] if stage == 2 else rl.at[stage, j]
        return pltpu.make_async_remote_copy(
            src_ref=sl.at[stage, j],
            dst_ref=landing,
            send_sem=rs_l.at[0, stage, j],
            recv_sem=rs_l.at[1, stage, j],
            device_id=left,
            device_id_type=MESH,
        )

    def to_right(stage, j):
        landing = last_hbm.at[pl.ds((2 + j) * TM, TM)] if stage == 2 else rr.at[stage, j]
        return pltpu.make_async_remote_copy(
            src_ref=sr.at[stage, j],
            dst_ref=landing,
            send_sem=rs_r.at[0, stage, j],
            recv_sem=rs_r.at[1, stage, j],
            device_id=right,
            device_id_type=MESH,
        )

    def far_tiles(j, carry):
        sl[0, j] = product_of(far, j * TM).astype(bf16)
        to_left(0, j).start()
        sr[0, j] = product_of(far, 2 * TM + j * TM).astype(bf16)
        to_right(0, j).start()
        return carry

    lax.fori_loop(0, 2, far_tiles, 0)

    def direct_tiles(j, carry):
        sl[1, j] = product_of(behind, 2 * TM + j * TM).astype(bf16)
        sr[1, j] = product_of(ahead, j * TM).astype(bf16)
        return carry

    lax.fori_loop(0, 2, direct_tiles, 0)

    def follow(stage, j, before, i):
        to_left(before, i).wait_send()
        to_left(stage, j).start()
        to_right(before, i).wait_send()
        to_right(stage, j).start()

    follow(1, 0, 0, 0)

    for i in range(NH):
        rows = slice(i * PS, (i + 1) * PS)
        terms[i : i + 1, :] -= te_s[0, i : i + 1, :] * jnp.sum(
            xt[rows, :].astype(f32) * r_s[0, rows, :], axis=0, keepdims=True
        )
    from_on = (row_i >= col_i).astype(f32).astype(bf16)
    suffix = [exact_dot(terms[:, k * Q : (k + 1) * Q], from_on) for k in range(2)]
    first, second = (jnp.broadcast_to(part[:, 0:1], (NH, N)) for part in suffix)
    head_lane = (
        lax.broadcasted_iota(jnp.int32, (NH, N), 0) == lax.broadcasted_iota(jnp.int32, (NH, N), 1)
    )
    tsum[...] = jnp.sum(jnp.where(head_lane, first + second, 0.0), axis=0, keepdims=True)

    def send_sum(o, carry):
        pltpu.make_async_remote_copy(
            src_ref=tsum,
            dst_ref=rt2.at[SEQ - o],
            send_sem=a_send.at[2],
            recv_sem=a_recv.at[2],
            device_id=(lax.rem(s + o, SEQ), sib[1]),
            device_id_type=MESH,
        ).start()
        return carry

    lax.fori_loop(1, SEQ, send_sum, 0)

    def next_tiles(j, carry):
        acc[0, j] = product_of(behind, j * TM)
        acc[1, j] = product_of(ahead, 2 * TM + j * TM)
        return carry

    lax.fori_loop(0, 2, next_tiles, 0)

    def own_tiles(j, carry):
        own[j] = product_of(z, j * TM)
        return carry

    lax.fori_loop(0, 4, own_tiles, 0)

    follow(1, 1, 0, 1)

    def add_later(o, total):
        return total + jnp.where(s + o < SEQ, rt2[o], 0.0)

    all_of(rt2.at[pl.ds(1, SEQ - 1)], 2).wait_recv()
    run_v[0] = lax.fori_loop(1, SEQ, add_later, jnp.zeros((1, N), f32))
    run_copy = to_sib(run_v.at[0], run_v.at[1], p_sem, 8)
    run_copy.start()

    for j in range(2):
        to_left(0, j).wait_recv()
        sl[2, j] = (acc[0, j] + rl[0, j].astype(f32)).astype(bf16)
        to_right(0, j).wait_recv()
        sr[2, j] = (acc[1, j] + rr[0, j].astype(f32)).astype(bf16)
        follow(2, j, 1, j)


    run_copy.wait()
    running = jnp.broadcast_to(run_v[1], (NH, N))
    running = jnp.sum(jnp.where(head_lane, running, 0.0), axis=1, keepdims=True)
    norm = 1.0 / math.sqrt(SEQ * TOK)
    gd_v[:, Q : 2 * Q] = (suffix[1] + running) * norm
    gd_v[:, 0:Q] = (suffix[0] + running + second[:, 0:1]) * norm

    outs = [pltpu.make_async_copy(gd_v, gd_hbm, out_sem.at[0])]
    outs[0].start()
    for j in range(2):
        to_right(1, j).wait_recv()
        o_v[j * TM : (j + 1) * TM, :] = (own[j] + rr[1, j].astype(f32)).astype(bf16)
        to_left(1, j).wait_recv()
        o_v[(2 + j) * TM : (3 + j) * TM, :] = (own[2 + j] + rl[1, j].astype(f32)).astype(bf16)
        for half in (j, 2 + j):
            rows = pl.ds(half * TM, TM)
            copy = pltpu.make_async_copy(o_v.at[rows], out_hbm.at[rows], out_sem.at[1 + half])
            copy.start()
            outs.append(copy)

    for i, ref in (
        (0, ra),
        (4, rt),
        (1, ob),
        (3, ob.at[pl.ds(1, SEQ - 1)]),
        (2, rt2.at[pl.ds(1, SEQ - 1)]),
    ):
        all_of(ref, i).wait_send()
    for j in range(2):
        to_left(2, j).wait_send()
        to_right(2, j).wait_send()
    for copy in outs:
        copy.wait()
    for j in range(2):
        to_left(2, j).wait_recv()
        to_right(2, j).wait_recv()


def hand_over(most, last, decays_in, out, decays):
    out[...] = (most[...].astype(f32) + last[...].astype(f32)).astype(bf16)
    decays[...] = decays_in[...]


def body(x_in, b_proj, c_proj, decay, d_skip, block_states, grad_out, w_x, w_b, w_c):
    any_spec = pl.BlockSpec(memory_space=pl.ANY)
    dma = pltpu.SemaphoreType.DMA
    most, last, decays = pl.pallas_call(
        kernel,
        out_shape=(
            jax.ShapeDtypeStruct((ROWS, TOK), bf16),
            jax.ShapeDtypeStruct((ROWS, TOK), bf16),
            jax.ShapeDtypeStruct((NH, TOK), f32),
        ),
        in_specs=[any_spec] * 10,
        out_specs=(any_spec, any_spec, any_spec),
        scratch_shapes=[
            pltpu.VMEM((TOK, HP), bf16),
            pltpu.VMEM((TOK, N), bf16),
            pltpu.VMEM((TOK, N), bf16),
            pltpu.VMEM((NH, TOK), f32),
            pltpu.VMEM((2 * HP, N), f32),
            pltpu.VMEM((TOK, HP), bf16),
            pltpu.VMEM((4, ROWS, 2 * KOWN), bf16),
            pltpu.VMEM((2 * KOWN, TOK), bf16),
            pltpu.VMEM((HP, TOK), bf16),
            pltpu.VMEM((HP, TOK), bf16),
            pltpu.VMEM((2, N, TOK), bf16),
            pltpu.VMEM((N, TOK), bf16),
            pltpu.VMEM((2, HP, TOK), bf16),
            pltpu.VMEM((HP, TOK), bf16),
            pltpu.VMEM((NH, TOK), f32),
            pltpu.VMEM((TOK, NH), f32),
            pltpu.VMEM((NH, TOK), f32),
            pltpu.VMEM((2, NH, TOK), f32),
            pltpu.VMEM((NH, N), f32),
            pltpu.VMEM((2, NH, N), f32),
            pltpu.VMEM((2, HP, N), f32),
            pltpu.VMEM((SEQ, SL, N), bf16),
            pltpu.VMEM((SEQ, SL, N), bf16),
            pltpu.VMEM((NH, 1, N), f32),
            pltpu.VMEM((SEQ, 1, N), f32),
            pltpu.VMEM((SEQ, SL, N), bf16),
            pltpu.VMEM((2, HP, N), bf16),
            pltpu.VMEM((2, HP, TOK), f32),
            pltpu.VMEM((2, N, TOK), f32),
            pltpu.VMEM((Q, Q), f32),
            pltpu.VMEM((Q, Q), f32),
            pltpu.VMEM((HP, Q), f32),
            pltpu.VMEM((2, HP, TOK), f32),
            pltpu.VMEM((NH, TOK), f32),
            pltpu.VMEM((SEQ, 1, N), f32),
            pltpu.VMEM((1, N), f32),
            pltpu.VMEM((2, 1, N), f32),
            pltpu.VMEM((3, 2, TM, TOK), bf16),
            pltpu.VMEM((2, 2, TM, TOK), bf16),
            pltpu.VMEM((3, 2, TM, TOK), bf16),
            pltpu.VMEM((2, 2, TM, TOK), bf16),
            pltpu.VMEM((4, TM, TOK), f32),
            pltpu.VMEM((2, 2, TM, TOK), f32),
            pltpu.VMEM((ROWS, TOK), bf16),
            pltpu.VMEM((NH, TOK), f32),
            pltpu.SMEM((NH,), f32),
            dma((10,)),
            dma((2, 3)),
            dma((2, 9)),
            dma((5,)),
            dma((5,)),
            dma((2, 3, 2)),
            dma((2, 3, 2)),
            dma((5,)),
        ],
        compiler_params=pltpu.CompilerParams(
            collective_id=0, has_side_effects=True, vmem_limit_bytes=60 * 2**20
        ),
    )(
        x_in,
        b_proj,
        c_proj,
        decay,
        d_skip,
        block_states.reshape(2 * HP, N),
        grad_out,
        w_x.reshape(4, 2, ROWS, HP),
        w_b.reshape(4, 2, ROWS, N),
        w_c.reshape(4, 2, ROWS, N),
    )
    return pl.pallas_call(
        hand_over,
        out_shape=(
            jax.ShapeDtypeStruct((ROWS, TOK), bf16),
            jax.ShapeDtypeStruct((NH, TOK), f32),
        ),
    )(most, last, decays)


def solution(mesh):
    return jax.shard_map(
        body,
        mesh=mesh,
        in_specs=(
            P("seq", "head"),
            P("seq", "head"),
            P("seq", "head"),
            P("head", "seq"),
            P("head"),
            P("seq", "head", None, None),
            P("seq", "head"),
            P(None, "head"),
            P(None, "head"),
            P(None, "head"),
        ),
        out_specs=(P("head", "seq"), P("head", "seq")),
        check_vma=False,
    )
```

```python
import math

import jax
import jax.numpy as jnp
from jax import lax
from jax.experimental import pallas as pl
from jax.experimental.pallas import tpu as pltpu
from jax.sharding import PartitionSpec as P

SEQ = 32
HEAD = 8
TOK = 512
Q = 256
NH = 8
PS = 64
N = 128
HP = NH * PS
KOWN = HP + 2 * N
ROWS = 512
TM = 128
SL = HP // SEQ

NZ, NX, NY = 2, 4, 4
STEPS = sorted(
    ((a, b, c) for a in range(NZ) for b in range(NX) for c in range(NY)),
    key=lambda t: -(min(t[0], NZ - t[0]) + min(t[1], NX - t[1]) + min(t[2], NY - t[2])),
)

MESH = pl.DeviceIdType.MESH
f32 = jnp.float32
bf16 = jnp.bfloat16

TN = (((0,), (0,)), ((), ()))
NT = (((1,), (1,)), ((), ()))


def dot(a, b, dims=(((1,), (0,)), ((), ()))):
    return lax.dot_general(a, b, dims, preferred_element_type=f32)


def split3(v):
    hi = v.astype(bf16).astype(f32)
    rest = v - hi
    mid = rest.astype(bf16).astype(f32)
    low = rest - mid
    return jnp.concatenate([hi, mid, low], axis=0).astype(bf16)


def exact_dot(v, mask):
    rows = v.shape[0]
    out = dot(split3(v), mask)
    return out[0:rows] + out[rows : 2 * rows] + out[2 * rows : 3 * rows]


def kernel(
    x_hbm, b_hbm, c_hbm, dec_hbm, skip_hbm, st_hbm, dy_hbm, wx_hbm, wb_hbm, wc_hbm,
    out_hbm, last_hbm, gd_hbm,
    x_v, b_v, c_v, dec_v, st_v, dy_v, w_v, g_v,
    xt, dyt, bt, ct, xte, dyfs, cum_s, cumt_s, fs_s, te_s, th0, th1,
    adj1, msg, ra, tt_s, rt, ob, a_v,
    gx, gb, wd, cb, yi, r_s, terms, rt2, tsum, run_v,
    sl, rl, sr, rr, own, acc, o_v, gd_v, skip_ref,
    load_sem, w_sem, p_sem, a_send, a_recv, rs_l, rs_r, out_sem,
):
    s = lax.axis_index("seq")
    h = lax.axis_index("head")
    z = h // 2
    core = lax.rem(h, 2)
    sib = (s, h + 1 - 2 * core)
    left = (s, lax.rem(h + HEAD - 2, HEAD))
    right = (s, lax.rem(h + 2, HEAD))

    at_z, at_x, at_y = s // (NX * NY), lax.rem(s // NY, NX), lax.rem(s, NY)

    def peer_at(step):
        return (
            lax.rem(at_z + step[0], NZ) * (NX * NY)
            + lax.rem(at_x + step[1], NX) * NY
            + lax.rem(at_y + step[2], NY)
        )

    def slot_at(step):
        a, b, c = ((size - i) % size for size, i in zip((NZ, NX, NY), step))
        return (a * NX + b) * NY + c

    def slot_of(d):
        return (
            lax.rem(d // (NX * NY) - at_z + NZ, NZ) * (NX * NY)
            + lax.rem(lax.rem(d // NY, NX) - at_x + NX, NX) * NY
            + lax.rem(lax.rem(d, NY) - at_y + NY, NY)
        )

    loads = [
        pltpu.make_async_copy(src, dst, load_sem.at[i])
        for i, (src, dst) in enumerate(
            (
                (dec_hbm, dec_v),
                (dy_hbm, dy_v),
                (c_hbm, c_v),
                (b_hbm, b_v),
                (x_hbm, x_v),
                (st_hbm, st_v),
                (wx_hbm.at[:, core], w_v.at[:, :, 0:HP]),
                (wb_hbm.at[:, core], w_v.at[:, :, HP : HP + N]),
                (wc_hbm.at[:, core], w_v.at[:, :, HP + N : KOWN]),
                (skip_hbm, skip_ref),
            )
        )
    ]
    for load in loads[:3]:
        load.start()

    barrier = pltpu.get_barrier_semaphore()

    for step in STEPS:
        other = (peer_at(step), sib[1])
        pl.semaphore_signal(barrier, inc=1, device_id=other, device_id_type=MESH)
        if any(step):
            other = (peer_at(step), h)
            pl.semaphore_signal(barrier, inc=1, device_id=other, device_id_type=MESH)
    for other in (left, right):
        pl.semaphore_signal(barrier, inc=1, device_id=other, device_id_type=MESH)

    for load in loads[3:]:
        load.start()

    row_i = lax.broadcasted_iota(jnp.int32, (Q, Q), 0)
    col_i = lax.broadcasted_iota(jnp.int32, (Q, Q), 1)

    loads[0].wait()
    upto = (row_i <= col_i).astype(f32).astype(bf16)
    log_decay = jnp.log(dec_v[...])
    for k in range(2):
        lanes = slice(k * Q, (k + 1) * Q)
        cum = exact_dot(log_decay[:, lanes], upto)
        cum_s[:, lanes] = cum
        fs_s[:, lanes] = jnp.exp(cum)
        last = jnp.broadcast_to(cum[:, Q - 1 : Q], (NH, Q))
        te_s[0, :, lanes] = jnp.exp(last - cum)
        (th0, th1.at[0])[k][...] = jnp.exp(last[:, 0:N])
    through = th0[...] * th1[0]
    for i in range(NH):
        tt_s[i] = through[i : i + 1, :]

    loads[1].wait()
    dyt[...] = dy_v[...].T
    for i in range(NH):
        rows = slice(i * PS, (i + 1) * PS)
        dyfs[rows, :] = (dyt[rows, :].astype(f32) * fs_s[i : i + 1, :]).astype(bf16)
    loads[2].wait()
    adj1[0] = dot(dyfs[:, Q : 2 * Q], c_v[Q : 2 * Q, :])
    adj0 = dot(dyfs[:, 0:Q], c_v[0:Q, :])
    for i in range(SEQ):
        rows = slice(i * SL, (i + 1) * SL)
        head = i * SL // PS
        msg[i] = (adj0[rows, :] + th0[head : head + 1, :] * adj1[0, rows, :]).astype(bf16)

    pl.semaphore_wait(barrier, 2 * SEQ + 1)

    for step in STEPS:
        to = peer_at(step)
        pltpu.make_async_remote_copy(
            src_ref=msg.at[to],
            dst_ref=ra.at[slot_at(step)],
            send_sem=a_send.at[0],
            recv_sem=a_recv.at[0],
            device_id=(to, sib[1]),
            device_id_type=MESH,
        ).start()
        pltpu.make_async_remote_copy(
            src_ref=tt_s.at[to // (SEQ // NH)],
            dst_ref=rt.at[slot_at(step)],
            send_sem=a_send.at[4],
            recv_sem=a_recv.at[4],
            device_id=(to, sib[1]),
            device_id_type=MESH,
        ).start()

    def to_sib(src, dst, sems, i):
        return pltpu.make_async_remote_copy(
            src_ref=src,
            dst_ref=dst,
            send_sem=sems.at[0, i],
            recv_sem=sems.at[1, i],
            device_id=sib,
            device_id_type=MESH,
        )

    w_copies = [
        to_sib(src.at[:, 1 - core], w_v.at[:, :, lo:hi], w_sem, i)
        for i, (src, lo, hi) in enumerate(
            (
                (wx_hbm, KOWN, KOWN + HP),
                (wb_hbm, KOWN + HP, KOWN + HP + N),
                (wc_hbm, KOWN + HP + N, 2 * KOWN),
            )
        )
    ]
    early = [
        to_sib(ref.at[0], ref.at[1], p_sem, i) for i, ref in enumerate((te_s, th1, adj1, bt, xte))
    ]
    for copy in w_copies:
        copy.start()

    loads[4].wait()
    xt[...] = x_v[...].T
    for i in range(NH):
        rows = slice(i * PS, (i + 1) * PS)
        xte[0, rows, :] = (xt[rows, :].astype(f32) * te_s[0, i : i + 1, :]).astype(bf16)
    loads[3].wait()
    bt[0] = b_v[...].T
    ct[...] = c_v[...].T
    cumt_s[...] = cum_s[...].T

    loads[5].wait()
    loads[9].wait()
    def block(k, carry):
        lanes = pl.ds(pl.multiple_of(k * Q, Q), Q)
        srows = pl.ds(pl.multiple_of(k * HP, HP), HP)
        c_k = c_v[lanes, :]
        bt_k = bt[0, :, lanes]
        ct_k = ct[:, lanes]
        s0 = st_v[srows, :].astype(bf16)
        cb[...] = dot(c_k, bt_k)
        yi[...] = dot(s0, ct_k)
        causal = row_i >= col_i
        for i in range(NH):
            rows = slice(i * PS, (i + 1) * PS)
            xh = xt[rows, lanes]
            dyh = dyt[rows, lanes]
            gaps = cumt_s[lanes, i : i + 1] - cum_s[i : i + 1, lanes]
            decay = jnp.exp(jnp.where(causal, gaps, -1e30))
            forward = (decay * cb[...]).astype(bf16)
            product = dot(dy_v[lanes, rows], xh)
            if i == 0:
                wd[...] = decay * product
            else:
                wd[...] += decay * product
            gx0 = dot(dyh, forward)
            y = dot(xh, forward, NT) + fs_s[i : i + 1, lanes] * yi[rows, :]
            dyf = dyh.astype(f32)
            terms[i : i + 1, lanes] = jnp.sum(dyf * y - xh.astype(f32) * gx0, axis=0, keepdims=True)
            gx[0, rows, lanes] = gx0 + skip_ref[i] * dyf
        decayed = wd[...].astype(bf16)
        gb[0, :, lanes] = dot(ct_k, decayed)
        gc = dot(bt_k, decayed, NT) + dot(s0, dyfs[:, lanes], TN)
        g_v[HP + N : KOWN, lanes] = gc.astype(bf16)
        return carry

    for copy in early:
        copy.start()
    lax.fori_loop(0, 2, block, 0)

    late = [
        to_sib(src, dst, p_sem, 5 + i)
        for i, (src, dst) in enumerate(
            (
                (gx.at[0], gx.at[1]),
                (gb.at[0], gb.at[1]),
                (g_v.at[pl.ds(HP + N, N)], g_v.at[pl.ds(KOWN + HP + N, N)]),
            )
        )
    ]
    for copy in late:
        copy.start()

    def all_of(ref, i):
        return pltpu.make_async_remote_copy(
            src_ref=ref,
            dst_ref=ref,
            send_sem=a_send.at[i],
            recv_sem=a_recv.at[i],
            device_id=sib,
            device_id_type=MESH,
        )

    all_of(ra, 0).wait_recv()
    all_of(rt, 4).wait_recv()

    def scan(step, cur):
        d = SEQ - 1 - step
        slot = slot_of(d)
        ob[d] = cur.astype(bf16)
        return ra[slot].astype(f32) + rt[slot] * cur

    cur = jnp.zeros((SL, N), f32)
    for step in range(SEQ):
        cur = scan(step, cur)
    own_rows = pl.ds(pl.multiple_of(s * SL, SL), SL)

    a_v[1, own_rows, :] = ob[s]
    for step in STEPS:
        to = peer_at(step)
        pltpu.make_async_remote_copy(
            src_ref=ob.at[to],
            dst_ref=a_v.at[0, own_rows],
            send_sem=a_send.at[1],
            recv_sem=a_recv.at[1],
            device_id=(to, sib[1]),
            device_id_type=MESH,
        ).start()
        if any(step):
            pltpu.make_async_remote_copy(
                src_ref=ob.at[to],
                dst_ref=a_v.at[1, own_rows],
                send_sem=a_send.at[3],
                recv_sem=a_recv.at[3],
                device_id=(to, h),
                device_id_type=MESH,
            ).start()

    all_of(a_v.at[0], 1).wait_recv()

    def with_adjoint(side):
        for k in (1, 0):
            lanes = slice(k * Q, (k + 1) * Q)
            later = a_v[side]
            if k == 0:
                later = jnp.concatenate(
                    [
                        (
                            adj1[side, i * PS : (i + 1) * PS, :]
                            + th1[side, i : i + 1, :]
                            * a_v[side, i * PS : (i + 1) * PS, :].astype(f32)
                        ).astype(bf16)
                        for i in range(NH)
                    ],
                    axis=0,
                )
            back = dot(later, bt[side, :, lanes])
            if side == 0:
                r_s[:, lanes] = back
            base = side * KOWN
            g_v[base + HP : base + HP + N, lanes] = (
                gb[side, :, lanes] + dot(later, xte[side, :, lanes], TN)
            ).astype(bf16)
            for i in range(NH):
                rows = slice(i * PS, (i + 1) * PS)
                g_v[base + i * PS : base + (i + 1) * PS, lanes] = (
                    gx[side, rows, lanes] + te_s[side, i : i + 1, lanes] * back[rows, :]
                ).astype(bf16)

    with_adjoint(0)
    for load in loads[6:9]:
        load.wait()
    for copy in early + late + w_copies:
        copy.wait()
    all_of(a_v.at[1, pl.ds(0, HP - SL)], 3).wait_recv()
    with_adjoint(1)

    def product_of(chunk, row):
        return dot(w_v[chunk, pl.ds(pl.multiple_of(row, TM), TM), :], g_v[...])

    ahead = lax.rem(z + 1, 4)
    behind = lax.rem(z + 3, 4)
    far = lax.rem(z + 2, 4)

    def to_left(stage, j):
        landing = last_hbm.at[pl.ds(j * TM, TM)] if stage == 2 else rl.at[stage, j]
        return pltpu.make_async_remote_copy(
            src_ref=sl.at[stage, j],
            dst_ref=landing,
            send_sem=rs_l.at[0, stage, j],
            recv_sem=rs_l.at[1, stage, j],
            device_id=left,
            device_id_type=MESH,
        )

    def to_right(stage, j):
        landing = last_hbm.at[pl.ds((2 + j) * TM, TM)] if stage == 2 else rr.at[stage, j]
        return pltpu.make_async_remote_copy(
            src_ref=sr.at[stage, j],
            dst_ref=landing,
            send_sem=rs_r.at[0, stage, j],
            recv_sem=rs_r.at[1, stage, j],
            device_id=right,
            device_id_type=MESH,
        )

    def far_tiles(j, carry):
        sl[0, j] = product_of(far, j * TM).astype(bf16)
        to_left(0, j).start()
        sr[0, j] = product_of(far, 2 * TM + j * TM).astype(bf16)
        to_right(0, j).start()
        return carry

    lax.fori_loop(0, 2, far_tiles, 0)

    def direct_tiles(j, carry):
        sl[1, j] = product_of(behind, 2 * TM + j * TM).astype(bf16)
        sr[1, j] = product_of(ahead, j * TM).astype(bf16)
        return carry

    lax.fori_loop(0, 2, direct_tiles, 0)

    def follow(stage, j, before, i):
        to_left(before, i).wait_send()
        to_left(stage, j).start()
        to_right(before, i).wait_send()
        to_right(stage, j).start()

    follow(1, 0, 0, 0)

    for i in range(NH):
        rows = slice(i * PS, (i + 1) * PS)
        terms[i : i + 1, :] -= te_s[0, i : i + 1, :] * jnp.sum(
            xt[rows, :].astype(f32) * r_s[rows, :], axis=0, keepdims=True
        )
    from_on = (row_i >= col_i).astype(f32).astype(bf16)
    suffix = [exact_dot(terms[:, k * Q : (k + 1) * Q], from_on) for k in range(2)]
    first, second = (jnp.broadcast_to(part[:, 0:1], (NH, N)) for part in suffix)
    head_lane = (
        lax.broadcasted_iota(jnp.int32, (NH, N), 0) == lax.broadcasted_iota(jnp.int32, (NH, N), 1)
    )
    tsum[...] = jnp.sum(jnp.where(head_lane, first + second, 0.0), axis=0, keepdims=True)

    def send_sum(o, carry):
        pltpu.make_async_remote_copy(
            src_ref=tsum,
            dst_ref=rt2.at[SEQ - o],
            send_sem=a_send.at[2],
            recv_sem=a_recv.at[2],
            device_id=(lax.rem(s + o, SEQ), sib[1]),
            device_id_type=MESH,
        ).start()
        return carry

    lax.fori_loop(1, SEQ, send_sum, 0)

    def next_tiles(j, carry):
        acc[0, j] = product_of(behind, j * TM)
        acc[1, j] = product_of(ahead, 2 * TM + j * TM)
        return carry

    lax.fori_loop(0, 2, next_tiles, 0)

    def own_tiles(j, carry):
        own[j] = product_of(z, j * TM)
        return carry

    lax.fori_loop(0, 4, own_tiles, 0)

    follow(1, 1, 0, 1)

    def add_later(o, total):
        return total + jnp.where(s + o < SEQ, rt2[o], 0.0)

    all_of(rt2.at[pl.ds(1, SEQ - 1)], 2).wait_recv()
    run_v[0] = lax.fori_loop(1, SEQ, add_later, jnp.zeros((1, N), f32))
    run_copy = to_sib(run_v.at[0], run_v.at[1], p_sem, 8)
    run_copy.start()

    for j in range(2):
        to_left(0, j).wait_recv()
        sl[2, j] = (acc[0, j] + rl[0, j].astype(f32)).astype(bf16)
        to_right(0, j).wait_recv()
        sr[2, j] = (acc[1, j] + rr[0, j].astype(f32)).astype(bf16)
        follow(2, j, 1, j)


    run_copy.wait()
    running = jnp.broadcast_to(run_v[1], (NH, N))
    running = jnp.sum(jnp.where(head_lane, running, 0.0), axis=1, keepdims=True)
    norm = 1.0 / math.sqrt(SEQ * TOK)
    gd_v[:, Q : 2 * Q] = (suffix[1] + running) * norm
    gd_v[:, 0:Q] = (suffix[0] + running + second[:, 0:1]) * norm

    outs = [pltpu.make_async_copy(gd_v, gd_hbm, out_sem.at[0])]
    outs[0].start()
    for j in range(2):
        to_right(1, j).wait_recv()
        o_v[j * TM : (j + 1) * TM, :] = (own[j] + rr[1, j].astype(f32)).astype(bf16)
        to_left(1, j).wait_recv()
        o_v[(2 + j) * TM : (3 + j) * TM, :] = (own[2 + j] + rl[1, j].astype(f32)).astype(bf16)
        for half in (j, 2 + j):
            rows = pl.ds(half * TM, TM)
            copy = pltpu.make_async_copy(o_v.at[rows], out_hbm.at[rows], out_sem.at[1 + half])
            copy.start()
            outs.append(copy)

    for i, ref in (
        (0, ra),
        (4, rt),
        (1, ob),
        (3, ob.at[pl.ds(1, SEQ - 1)]),
        (2, rt2.at[pl.ds(1, SEQ - 1)]),
    ):
        all_of(ref, i).wait_send()
    for j in range(2):
        to_left(2, j).wait_send()
        to_right(2, j).wait_send()
    for copy in outs:
        copy.wait()
    for j in range(2):
        to_left(2, j).wait_recv()
        to_right(2, j).wait_recv()


def hand_over(most, last, decays_in, out, decays):
    out[...] = (most[...].astype(f32) + last[...].astype(f32)).astype(bf16)

    @pl.when(pl.program_id(0) == 0)
    def _():
        decays[...] = decays_in[...]


def body(x_in, b_proj, c_proj, decay, d_skip, block_states, grad_out, w_x, w_b, w_c):
    any_spec = pl.BlockSpec(memory_space=pl.ANY)
    dma = pltpu.SemaphoreType.DMA
    most, last, decays = pl.pallas_call(
        kernel,
        out_shape=(
            jax.ShapeDtypeStruct((ROWS, TOK), bf16),
            jax.ShapeDtypeStruct((ROWS, TOK), bf16),
            jax.ShapeDtypeStruct((NH, TOK), f32),
        ),
        in_specs=[any_spec] * 10,
        out_specs=(any_spec, any_spec, any_spec),
        scratch_shapes=[
            pltpu.VMEM((TOK, HP), bf16),
            pltpu.VMEM((TOK, N), bf16),
            pltpu.VMEM((TOK, N), bf16),
            pltpu.VMEM((NH, TOK), f32),
            pltpu.VMEM((2 * HP, N), f32),
            pltpu.VMEM((TOK, HP), bf16),
            pltpu.VMEM((4, ROWS, 2 * KOWN), bf16),
            pltpu.VMEM((2 * KOWN, TOK), bf16),
            pltpu.VMEM((HP, TOK), bf16),
            pltpu.VMEM((HP, TOK), bf16),
            pltpu.VMEM((2, N, TOK), bf16),
            pltpu.VMEM((N, TOK), bf16),
            pltpu.VMEM((2, HP, TOK), bf16),
            pltpu.VMEM((HP, TOK), bf16),
            pltpu.VMEM((NH, TOK), f32),
            pltpu.VMEM((TOK, NH), f32),
            pltpu.VMEM((NH, TOK), f32),
            pltpu.VMEM((2, NH, TOK), f32),
            pltpu.VMEM((NH, N), f32),
            pltpu.VMEM((2, NH, N), f32),
            pltpu.VMEM((2, HP, N), f32),
            pltpu.VMEM((SEQ, SL, N), bf16),
            pltpu.VMEM((SEQ, SL, N), bf16),
            pltpu.VMEM((NH, 1, N), f32),
            pltpu.VMEM((SEQ, 1, N), f32),
            pltpu.VMEM((SEQ, SL, N), bf16),
            pltpu.VMEM((2, HP, N), bf16),
            pltpu.VMEM((2, HP, TOK), f32),
            pltpu.VMEM((2, N, TOK), f32),
            pltpu.VMEM((Q, Q), f32),
            pltpu.VMEM((Q, Q), f32),
            pltpu.VMEM((HP, Q), f32),
            pltpu.VMEM((HP, TOK), f32),
            pltpu.VMEM((NH, TOK), f32),
            pltpu.VMEM((SEQ, 1, N), f32),
            pltpu.VMEM((1, N), f32),
            pltpu.VMEM((2, 1, N), f32),
            pltpu.VMEM((3, 2, TM, TOK), bf16),
            pltpu.VMEM((2, 2, TM, TOK), bf16),
            pltpu.VMEM((3, 2, TM, TOK), bf16),
            pltpu.VMEM((2, 2, TM, TOK), bf16),
            pltpu.VMEM((4, TM, TOK), f32),
            pltpu.VMEM((2, 2, TM, TOK), f32),
            pltpu.VMEM((ROWS, TOK), bf16),
            pltpu.VMEM((NH, TOK), f32),
            pltpu.SMEM((NH,), f32),
            dma((10,)),
            dma((2, 3)),
            dma((2, 9)),
            dma((5,)),
            dma((5,)),
            dma((2, 3, 2)),
            dma((2, 3, 2)),
            dma((5,)),
        ],
        compiler_params=pltpu.CompilerParams(
            collective_id=0, has_side_effects=True, vmem_limit_bytes=60 * 2**20
        ),
    )(
        x_in,
        b_proj,
        c_proj,
        decay,
        d_skip,
        block_states.reshape(2 * HP, N),
        grad_out,
        w_x.reshape(4, 2, ROWS, HP),
        w_b.reshape(4, 2, ROWS, N),
        w_c.reshape(4, 2, ROWS, N),
    )
    block = pl.BlockSpec((ROWS // 2, TOK), lambda i: (i, 0))
    whole = pl.BlockSpec((NH, TOK), lambda i: (0, 0))
    return pl.pallas_call(
        hand_over,
        out_shape=(
            jax.ShapeDtypeStruct((ROWS, TOK), bf16),
            jax.ShapeDtypeStruct((NH, TOK), f32),
        ),
        grid=(2,),
        in_specs=(block, block, whole),
        out_specs=(block, whole),
    )(most, last, decays)


def solution(mesh):
    return jax.shard_map(
        body,
        mesh=mesh,
        in_specs=(
            P("seq", "head"),
            P("seq", "head"),
            P("seq", "head"),
            P("head", "seq"),
            P("head"),
            P("seq", "head", None, None),
            P("seq", "head"),
            P(None, "head"),
            P(None, "head"),
            P(None, "head"),
        ),
        out_specs=(P("head", "seq"), P("head", "seq")),
        check_vma=False,
    )
```
